32 devices in a mesh: groups: 2 (over x), pool: 16 (over z, y, core).
Axes of the slice: x: 2, y: 2, z: 4, core: 2. Of those that a mesh axis runs over, the one named last changes fastest.
Arguments:
- queries: bfloat16 [32, 1024, 2304], P(('groups', 'pool')), parts along dimension 0, may hold values from -80 to 80
- pool_cache: bfloat16 [3072, 9216], P(('groups', 'pool')), parts along dimension 0, may hold values from -5 to 5
- new_raw: bfloat16 [128, 9216], P(('groups', 'pool')), parts along dimension 0, may hold values from -700 to 700
- norm_gain: bfloat16 [512], replicated, may hold values from 0.5 to 1.5
- hit_pages: int32 [32], P('groups'), parts along dimension 0, may hold values from 36 to 48, as said below
- prompt_len: int32 [32], P('groups'), parts along dimension 0, may hold values from 592 to 832, as said below
- page_holder: int32 [32, 48], P('groups'), parts along dimension 0, may hold values from 0 to 15, as said below
- page_slot: int32 [32, 48], P('groups'), parts along dimension 0, may hold values from 0 to 95
- page_owner: int32 [32, 52, 1], P('groups'), parts along dimension 0, may hold values from 0 to 15; in each aligned block of 52 rows (0 to 51, 52 to 103, ..., all dimensions but the last counted through in order) at most 4 rows name the same one
Outputs:
- context: bfloat16 [32, 1024, 2048], P(('groups', 'pool')), parts along dimension 0
- delivered: bfloat16 [2048, 9216], P(('groups', 'pool')), parts along dimension 0
The draws below stay inside these ranges and needn't reach their ends.
There are 2 independent parts, one for each index of `groups`. The reference program is written for one: setup_inputs(seed, part) draws one part's arguments, and reference() takes and returns one part's arrays. A program takes and returns all parts, laid end to end along the dimension named above; an argument that names none is the same for every part. Nothing has to cross between parts.
Inputs may be any that keep to these rules, and one draw needn't show every extreme that they name: `hit_pages`: at least three quarters of 48; 48 in some prompt. prompt_len - 16 * hit_pages lies between a quarter of 64 and 64; one prompt has both 48 hit pages and 64 miss tokens. `page_holder`: the pages of one prompt lie in runs of at most 6 consecutive pages, each run on another pool device, so no device holds more than 6 pages of one prompt. `page_owner`: among the 52 pages of one prompt no owner is named more than 4 times.
All inputs are finite; a program needn't handle non-finite values.
Results may differ from the reference program's by a relative error of at most 0.0047.
Values may be sent and summed in bfloat16 or wider, within the bound.
A program may use at most 192 MiB of HBM per device.

```python
import math
import jax
import jax.numpy as jnp
import numpy as np
from jax import lax

HEADS = 64
LATENT_WIDTH = 512
ROPE = 64
PAGE = 16
TPW = 16
MISS = 64
HITP = 48
POOL_DEV = 96
PROMPTS = 16
HEAD_DEV = 4
TP_GROUPS = 1
NEWP = 4
CAP = 6
PUSH_CAP = 4
N_POOL = 16


def length_pair(key):
    key = jax.random.fold_in(key, 11)
    hit_key, miss_key, pick_key = jax.random.split(key, 3)
    hits = jax.random.randint(hit_key, (PROMPTS,), HITP * 3 // 4, HITP + 1)
    misses = jax.random.randint(miss_key, (PROMPTS,), MISS // 4, MISS + 1)
    chosen = jax.random.randint(pick_key, (), 0, PROMPTS)
    hits = hits.at[chosen].set(HITP)
    misses = misses.at[chosen].set(MISS)
    return (hits.astype(jnp.int32), misses.astype(jnp.int32))


def holder_table(key):
    key = jax.random.fold_in(key, 23)
    order_keys = jax.random.split(key, PROMPTS + 1)
    orders = jax.vmap(lambda subkey: jax.random.permutation(subkey, N_POOL))(order_keys[:PROMPTS])
    shifts = jax.random.randint(order_keys[PROMPTS], (PROMPTS, 1), 0, CAP)
    run_index = (jnp.arange(HITP)[None, :] + shifts) // CAP
    return jnp.take_along_axis(orders, run_index, axis=1).astype(jnp.int32)


def slot_table(key):
    key = jax.random.fold_in(key, 37)
    return jax.random.randint(key, (PROMPTS, HITP), 0, POOL_DEV).astype(jnp.int32)


def cache_base(key):
    key = jax.random.fold_in(key, 41)
    values = jax.random.normal(key, (N_POOL * POOL_DEV, PAGE, LATENT_WIDTH + ROPE), jnp.float32)
    return jnp.clip(values, -5.0, 5.0)


def device_layout(values):
    shaped = values.reshape(TP_GROUPS, TPW, MISS, TPW, HEAD_DEV, LATENT_WIDTH + ROPE).transpose(0, 3, 1, 2, 4, 5)
    return shaped.reshape(PROMPTS, TPW * MISS, HEAD_DEV * (LATENT_WIDTH + ROPE)).astype(jnp.bfloat16)


def draw_hit_pages(key, part):
    return length_pair(key)[0]


def draw_prompt_len(key, part):
    hits, misses = length_pair(key)
    return (hits * PAGE + misses).astype(jnp.int32)


def draw_page_holder(key, part):
    return holder_table(key)


def draw_page_slot(key, part):
    return slot_table(key)


def draw_pool_cache(key, part):
    values = cache_base(key)
    return values.reshape(N_POOL * POOL_DEV, PAGE * (LATENT_WIDTH + ROPE)).astype(jnp.bfloat16)


def draw_queries(key, part):
    base_key = jax.random.fold_in(key, 53)
    shape_all = (PROMPTS, MISS, HEADS, LATENT_WIDTH + ROPE)
    values = jnp.clip(jax.random.normal(base_key, shape_all, jnp.float32), -4.0, 4.0) * 0.6
    return device_layout(values)


def draw_new_raw(key, part):
    key = jax.random.fold_in(key, 67)
    base_key, row_key, column_key = jax.random.split(key, 3)
    row_total = PROMPTS * MISS
    features = LATENT_WIDTH + ROPE
    values = jnp.clip(jax.random.normal(base_key, (row_total, features), jnp.float32), -4.0, 4.0)
    spread = math.log(10.0)
    row_scale = jnp.exp(jax.random.uniform(row_key, (row_total, 1), jnp.float32, 0.0, spread))
    column_scale = jnp.exp(jax.random.uniform(column_key, (1, features), jnp.float32, 0.0, spread))
    latent_mask = jnp.arange(features)[None, :] < LATENT_WIDTH
    values = jnp.where(latent_mask, values * row_scale * column_scale, values)
    return values.reshape(PROMPTS * NEWP, PAGE * features).astype(jnp.bfloat16)


def routed_block(own_key, own, number, rows, amount, top, most, skew):
    ranking = jax.random.permutation(own_key, amount)
    packed, usual = portions_of(amount, rows * top, most, skew, True), portions_of(amount, rows * top, most, skew, False)
    places = jnp.arange(amount)

    def named(lengths, rotation):
        used = int((lengths > 0).sum())
        fixed = max(1, used // 4)
        passed = fixed + (places - fixed + rotation * (used - fixed)) % max(1, amount - fixed)
        return jnp.zeros((amount,), jnp.int32).at[ranking[jnp.where(places < fixed, places, passed)]].set(jnp.asarray(lengths, jnp.int32))

    lengths = jnp.where(number % 4 == 0, named(packed, number // 4), named(usual, number - number // 4 - 1))
    mixed = jax.random.permutation(jax.random.fold_in(own, 3), amount)
    giver, taker = mixed[0:amount // 2 * 2:2], mixed[1:amount // 2 * 2:2]
    margin = jnp.minimum(lengths[giver] - 1, most - lengths[taker]) // 2
    margin = jnp.where((giver == ranking[0]) | (taker == ranking[0]) | (lengths[taker] == 0), 0, jnp.maximum(margin, 0))
    passed = jax.random.randint(jax.random.fold_in(own, 4), (amount // 2,), 0, 1 << 20) % (margin + 1)
    lengths = lengths.at[giver].add(-passed).at[taker].add(passed)
    labels = jnp.searchsorted(jnp.cumsum(lengths), jnp.arange(rows * top), side="right").astype(jnp.int32)
    listing = labels.reshape(top, rows).T
    listing = listing[jax.random.permutation(jax.random.fold_in(own, 1), rows)]
    rotation = jax.random.randint(jax.random.fold_in(own, 2), (rows, 1), 0, top)
    return jnp.take_along_axis(listing, (jnp.arange(top)[None, :] + rotation) % top, axis=1)


def portions_of(amount, total, bound, lean, full):
    weights = [(1 << 20) // math.isqrt(rank ** lean) + 1 for rank in range(1, amount + 1)]
    largest = bound if full else min(bound, max(-(-total // amount), total * weights[0] // sum(weights)))
    least = 1 if total - largest >= amount - 1 else 0
    counts, surplus = [largest] + [least] * (amount - 1), total - largest - least * (amount - 1)
    while surplus > 0:
        movable = [i for i in range(1, amount) if counts[i] < largest] or [i for i in range(1, amount) if counts[i] < bound]
        pool, budget = sum([weights[i] for i in movable]), surplus
        for i in movable:
            extra = min(bound - counts[i], max(1, budget * weights[i] // pool), surplus)
            counts[i] = counts[i] + extra
            surplus = surplus - extra
    return np.array(counts)


def setup_inputs(seed: int = 0, part: int = 0) -> dict:
    arg_keys = jax.random.split(jax.random.key(seed), 10)
    part_keys = jax.random.split(jax.random.fold_in(arg_keys[9], part), 10)
    queries = draw_queries(jax.random.fold_in(jax.random.fold_in(arg_keys[9], part), 71), part)
    pool_cache = draw_pool_cache(jax.random.fold_in(jax.random.fold_in(arg_keys[9], part), 71), part)
    new_raw = draw_new_raw(jax.random.fold_in(jax.random.fold_in(arg_keys[9], part), 71), part)
    norm_gain = jnp.clip(1.0 + 0.1 * jax.random.normal(arg_keys[3], (LATENT_WIDTH,), jnp.float32), 0.5, 1.5).astype(jnp.bfloat16)
    hit_pages = draw_hit_pages(jax.random.fold_in(jax.random.fold_in(arg_keys[9], part), 71), part)
    prompt_len = draw_prompt_len(jax.random.fold_in(jax.random.fold_in(arg_keys[9], part), 71), part)
    page_holder = draw_page_holder(jax.random.fold_in(jax.random.fold_in(arg_keys[9], part), 71), part)
    page_slot = draw_page_slot(jax.random.fold_in(jax.random.fold_in(arg_keys[9], part), 71), part)
    page_owner_keys = jax.random.split(jax.random.fold_in(part_keys[8], 1), PROMPTS * (HITP + NEWP) // (HITP + NEWP))
    page_owner_turns = jax.random.permutation(jax.random.fold_in(part_keys[8], 3), PROMPTS * (HITP + NEWP) // (HITP + NEWP))
    page_owner = jax.vmap(lambda own, number: routed_block(jax.random.fold_in(part_keys[8], 2), own, number, HITP + NEWP, N_POOL, 1, PUSH_CAP, 1))(page_owner_keys, page_owner_turns).reshape((PROMPTS, HITP + NEWP, 1))
    return {"queries": queries, "pool_cache": pool_cache, "new_raw": new_raw, "norm_gain": norm_gain, "hit_pages": hit_pages, "prompt_len": prompt_len, "page_holder": page_holder, "page_slot": page_slot, "page_owner": page_owner}


score_scale = 0.07216878364870323
rope_base = 10000.0
norm_eps = 1e-06

def rope_tables(positions, rotary_width):
    half_width = rotary_width // 2
    frequencies = rope_base ** (jnp.arange(half_width).astype(jnp.float32) * (-2.0 / rotary_width))
    angles = positions.astype(jnp.float32)[:, None] * frequencies[None, :]
    return (jnp.cos(angles), jnp.sin(angles))

def rotate(values, cosine, sine_table):
    half_width = values.shape[-1] // 2
    lower = values[..., :half_width]
    upper = values[..., half_width:]
    return jnp.concatenate([lower * cosine - upper * sine_table, upper * cosine + lower * sine_table], axis=-1)

def fresh_keys(raw_rows, norm_gain, hit_count, miss_count):
    latent = raw_rows[:, :LATENT_WIDTH]
    rotary = raw_rows[:, LATENT_WIDTH:]
    mean_square = lax.optimization_barrier(jnp.mean(latent * latent, axis=1, keepdims=True))
    normed = latent * lax.rsqrt(mean_square + norm_eps) * norm_gain.astype(jnp.float32)[None, :]
    row_steps = jnp.arange(raw_rows.shape[0]).astype(jnp.int32)
    cosine, sine_table = rope_tables(hit_count * PAGE + row_steps, ROPE)
    turned = rotate(rotary, cosine, sine_table)
    joined = jnp.concatenate([normed, turned], axis=1)
    return jnp.where((row_steps < miss_count)[:, None], joined, 0.0).astype(jnp.bfloat16)

def attend(query_rows, latent_keys, key_valid_mask, hit_count, miss_count):
    row_count = query_rows.shape[0]
    features = latent_keys.shape[1]
    cached_rows = key_valid_mask.shape[0]
    row_steps = jnp.arange(row_count).astype(jnp.int32)
    heads_in = query_rows.astype(jnp.float32).reshape(row_count, -1, features)
    cosine, sine_table = rope_tables(hit_count * PAGE + row_steps, ROPE)
    turned = rotate(heads_in[..., LATENT_WIDTH:], cosine[:, None, :], sine_table[:, None, :])
    head_queries = jnp.concatenate([heads_in[..., :LATENT_WIDTH], turned], axis=2).astype(jnp.bfloat16)
    scores = jnp.einsum('qhd,kd->hqk', head_queries.astype(jnp.float32), latent_keys.astype(jnp.float32)) * score_scale
    fresh_steps = jnp.arange(latent_keys.shape[0] - cached_rows).astype(jnp.int32)
    fresh_live = (fresh_steps[None, :] <= row_steps[:, None]) & (fresh_steps[None, :] < miss_count)
    allowed = jnp.concatenate([jnp.broadcast_to(key_valid_mask[None, :], (row_count, cached_rows)), fresh_live], axis=1)
    scores = jnp.where(allowed[None, :, :], scores, -jnp.inf)
    row_max = lax.optimization_barrier(jnp.max(scores, axis=2, keepdims=True))
    weights = jnp.exp(scores - row_max)
    attention_weights = (weights / lax.optimization_barrier(jnp.sum(weights, axis=2, keepdims=True))).astype(jnp.bfloat16)
    context = jnp.einsum('hqk,kd->qhd', attention_weights.astype(jnp.float32), latent_keys[:, :LATENT_WIDTH].astype(jnp.float32))
    context = jnp.where((row_steps < miss_count)[:, None, None], context, 0.0)
    return context.reshape(row_count, -1).astype(jnp.bfloat16)

def reference(queries, pool_cache, new_raw, norm_gain, hit_pages, prompt_len, page_holder, page_slot, page_owner):
    prompts = hit_pages.shape[0]
    groups_tp = prompts // TPW
    features = pool_cache.shape[1] // PAGE
    misses = prompt_len - PAGE * hit_pages
    raw_rows = new_raw.astype(jnp.float32).reshape(prompts, NEWP * PAGE, features)
    new_keys = jax.vmap(fresh_keys, in_axes=(0, None, 0, 0))(raw_rows, norm_gain, hit_pages, misses)
    query_blocks = queries.reshape(groups_tp, TPW, TPW, MISS, HEAD_DEV * features)
    query_blocks = query_blocks.transpose(0, 2, 3, 1, 4).reshape(prompts, MISS, HEADS * features)
    page_index = (page_holder * POOL_DEV + page_slot).astype(jnp.int32)
    page_steps = jnp.arange(HITP).astype(jnp.int32)

    def one_prompt(inputs):
        query_rows, own_keys, hit_count, miss_count, local_owner_index = inputs
        cached = pool_cache[local_owner_index].reshape(HITP * PAGE, features)
        key_valid_mask = jnp.repeat(page_steps < hit_count, PAGE)
        latent_keys = jnp.concatenate([cached, own_keys], axis=0)
        return attend(query_rows, latent_keys, key_valid_mask, hit_count, miss_count)
    context = lax.map(one_prompt, (query_blocks, new_keys, hit_pages, misses, page_index))
    context = context.reshape(groups_tp, TPW, MISS, TPW, HEAD_DEV * LATENT_WIDTH)
    context = context.transpose(0, 3, 1, 2, 4).reshape(prompts, TPW * MISS, HEAD_DEV * LATENT_WIDTH)
    total = HITP + NEWP
    hit_rows = pool_cache[page_index.reshape(-1)].reshape(prompts, HITP, PAGE * features)
    new_rows = new_keys.reshape(prompts, NEWP, PAGE * features)
    pages = jnp.concatenate([hit_rows, new_rows], axis=1).reshape(prompts * total, PAGE * features)
    owners = page_owner[:, :, 0]
    new_steps = jnp.arange(NEWP).astype(jnp.int32)
    hit_live = page_steps[None, :] < hit_pages[:, None]
    new_live = new_steps[None, :] * PAGE < misses[:, None]
    page_live = jnp.concatenate([hit_live, new_live], axis=1)
    all_steps = jnp.arange(total).astype(jnp.int32)
    earlier = all_steps[:, None] < all_steps[None, :]
    same_owner = (owners[:, :, None] == owners[:, None, :]) & page_live[:, :, None] & earlier[None, :, :]
    page_rank = lax.optimization_barrier(jnp.sum(same_owner.astype(jnp.int32), axis=1))
    prompt_steps = jnp.arange(prompts).astype(jnp.int32)
    target = (owners * prompts + prompt_steps[:, None]) * PUSH_CAP + page_rank
    slots_all = prompts * prompts * PUSH_CAP
    target = jnp.where(page_live, target, slots_all).reshape(-1).astype(jnp.int32)
    delivered = jnp.zeros((slots_all, PAGE * features), jnp.bfloat16).at[target].set(pages, mode='drop')
    return (context, delivered)
```

```python
import functools

import jax
import jax.numpy as jnp
from jax import lax
from jax.experimental import pallas as pl
from jax.experimental.pallas import tpu as pltpu
from jax.sharding import PartitionSpec as P

LATENT_WIDTH = 512
ROPE = 64
PAGE = 16
TPW = 16
PACK = 128
MESH = pl.DeviceIdType.MESH


score_scale = 0.07216878364870323
rope_base = 10000.0
norm_eps = 1e-06


def rope_tables(positions, rotary_width):
    half_width = rotary_width // 2
    frequencies = rope_base ** (jnp.arange(half_width).astype(jnp.float32) * (-2.0 / rotary_width))
    angles = positions.astype(jnp.float32)[:, None] * frequencies[None, :]
    return (jnp.cos(angles), jnp.sin(angles))


def rotate(values, cosine, sine_table):
    half_width = values.shape[-1] // 2
    lower = values[..., :half_width]
    upper = values[..., half_width:]
    return jnp.concatenate(
        [lower * cosine - upper * sine_table, upper * cosine + lower * sine_table], axis=-1
    )


def fresh_keys(raw_rows, norm_gain, hit_count, miss_count):
    latent = raw_rows[:, :LATENT_WIDTH]
    rotary = raw_rows[:, LATENT_WIDTH:]
    mean_square = jnp.mean(latent * latent, axis=1, keepdims=True)
    normed = latent * lax.rsqrt(mean_square + norm_eps) * norm_gain.astype(jnp.float32)[None, :]
    row_steps = jnp.arange(raw_rows.shape[0])
    cosine, sine_table = rope_tables(hit_count * PAGE + row_steps, ROPE)
    turned = rotate(rotary, cosine, sine_table)
    joined = jnp.concatenate([normed, turned], axis=1)
    return jnp.where((row_steps < miss_count)[:, None], joined, 0.0).astype(jnp.bfloat16)


def pick_rows(slot_position, valid_rows, rows, slot_total):
    selector = (jnp.arange(slot_total)[:, None] == slot_position[None, :]) & valid_rows[None, :]
    return jnp.dot(selector.astype(jnp.bfloat16), rows, preferred_element_type=jnp.float32).astype(
        jnp.bfloat16
    )


def turn_queries(query_rows, hits):
    batch, miss_rows = (query_rows.shape[0], query_rows.shape[1])
    row_steps = jnp.arange(miss_rows)
    positions = (hits[:, None] * PAGE + row_steps[None, :]).reshape(-1)
    cosine, sine_table = rope_tables(positions, ROPE)
    cosine = cosine.reshape(batch, miss_rows, 1, -1)
    sine_table = sine_table.reshape(batch, miss_rows, 1, -1)
    turned = rotate(query_rows[..., LATENT_WIDTH:].astype(jnp.float32), cosine, sine_table).astype(
        jnp.bfloat16
    )
    by_head = lambda value: value.transpose(0, 2, 1, 3).reshape(batch, -1, value.shape[-1])
    latent = by_head(query_rows[..., :LATENT_WIDTH])
    rotary = by_head(turned)
    blank = jnp.zeros_like(rotary)
    paired = jnp.concatenate(
        [jnp.concatenate([rotary, blank], axis=2), jnp.concatenate([blank, rotary], axis=2)], axis=1
    )
    return latent, paired


def pack_keys(keys):
    rotary = keys[:, LATENT_WIDTH:]
    spare = PACK * (LATENT_WIDTH // ROPE) - keys.shape[0]
    rotary = jnp.concatenate([rotary, jnp.zeros((spare, ROPE), keys.dtype)], axis=0)
    packed = rotary.reshape(-1, PACK, ROPE).transpose(1, 0, 2).reshape(PACK, LATENT_WIDTH)
    return jnp.concatenate([keys[:, :LATENT_WIDTH], packed], axis=0)


def gather_body(own, out, local_sem, up_sem, down_sem, y_sem, core_sem, recv_sem):
    me = lax.axis_index("pool")
    member = lax.rem(me, TPW)
    base = me - member
    z, y, c = member // 4, lax.rem(member // 2, 2), lax.rem(member, 2)

    def slot_of(zz, yy, cc):
        return zz * 4 + yy * 2 + cc

    across = base + slot_of(z, 1 - y, c)
    twin = base + slot_of(z, y, 1 - c)
    above = base + slot_of(lax.rem(z + 1, 4), y, c)
    below = base + slot_of(lax.rem(z + 3, 4), y, c)
    has_up, has_down = z < 3, z > 0

    barrier = pltpu.get_barrier_semaphore()
    pl.semaphore_signal(barrier, inc=1, device_id={"pool": across}, device_id_type=MESH)
    pl.semaphore_signal(barrier, inc=1, device_id={"pool": twin}, device_id_type=MESH)

    @pl.when(has_up)
    def _():
        pl.semaphore_signal(barrier, inc=1, device_id={"pool": above}, device_id_type=MESH)

    @pl.when(has_down)
    def _():
        pl.semaphore_signal(barrier, inc=1, device_id={"pool": below}, device_id_type=MESH)

    pl.semaphore_wait(barrier, 2 + has_up.astype(jnp.int32) + has_down.astype(jnp.int32))

    def copy(zz, yy, cc, sem, device, first):
        slot = slot_of(zz, yy, cc)
        return pltpu.make_async_remote_copy(
            src_ref=own if first else out.at[slot],
            dst_ref=out.at[slot],
            send_sem=sem,
            recv_sem=recv_sem.at[slot],
            device_id={"pool": device},
            device_id_type=MESH,
        )

    def arrive(zz, yy, cc):
        copy(zz, yy, cc, core_sem.at[0], twin, False).wait_recv()

    def column(zz, act, up, down, first=False):
        if up:
            @pl.when(has_up)
            def _():
                act(copy(zz, y, c, up_sem.at[zz], above, first))
        if down:
            @pl.when(has_down)
            def _():
                act(copy(zz, y, c, down_sem.at[zz], below, first))
        act(copy(zz, y, c, y_sem.at[zz], across, first))
        act(copy(zz, y, c, core_sem.at[zz * 2 + y], twin, first))

    def side(zz):
        arrive(zz, 1 - y, c)
        copy(zz, 1 - y, c, core_sem.at[zz * 2 + 1 - y], twin, False).start()

    def sides(step):
        @pl.when(z >= step)
        def _():
            side(z - step)
        if step:
            @pl.when(z + step <= 3)
            def _():
                side(z + step)

    start = lambda item: item.start()
    mine = pltpu.make_async_copy(own, out.at[member], local_sem)
    mine.start()
    column(z, start, True, True, True)
    for step in range(1, 4):
        @pl.when(z >= step)
        def _():
            arrive(z - step, y, c)
            column(z - step, start, True, False)

        @pl.when(z + step <= 3)
        def _():
            arrive(z + step, y, c)
            column(z + step, start, False, True)

        sides(step - 1)
    sides(3)
    for zz in range(4):
        for yy in range(2):
            arrive(zz, yy, 1 - c)
    ended = lambda item: item.wait_send()
    mine.wait()
    column(z, ended, True, True, True)
    copy(z, 1 - y, c, core_sem.at[z * 2 + 1 - y], twin, False).wait_send()
    for step in range(1, 4):
        @pl.when(z >= step)
        def _():
            column(z - step, ended, True, False)
            copy(z - step, 1 - y, c, core_sem.at[(z - step) * 2 + 1 - y], twin, False).wait_send()

        @pl.when(z + step <= 3)
        def _():
            column(z + step, ended, False, True)
            copy(z + step, 1 - y, c, core_sem.at[(z + step) * 2 + 1 - y], twin, False).wait_send()


def gather_keys(own):
    return pl.pallas_call(
        gather_body,
        out_shape=jax.ShapeDtypeStruct((TPW,) + own.shape, own.dtype),
        in_specs=[pl.BlockSpec(memory_space=pl.ANY)],
        out_specs=pl.BlockSpec(memory_space=pl.ANY),
        scratch_shapes=[
            pltpu.SemaphoreType.DMA,
            pltpu.SemaphoreType.DMA((4,)),
            pltpu.SemaphoreType.DMA((4,)),
            pltpu.SemaphoreType.DMA((4,)),
            pltpu.SemaphoreType.DMA((8,)),
            pltpu.SemaphoreType.DMA((TPW,)),
        ],
        compiler_params=pltpu.CompilerParams(collective_id=0, has_side_effects=True),
    )(own)


def attend_one(latent_queries, paired_queries, keys, hits, misses, key_count, miss_rows):
    rows = latent_queries.shape[0]
    cached_rows = key_count - miss_rows
    contract = (((1,), (1,)), ((), ()))
    latent_keys = keys[:key_count, :]
    scores = lax.dot_general(
        latent_queries, latent_keys, contract, preferred_element_type=jnp.float32
    )
    parts = []
    for pair in range(LATENT_WIDTH // 128):
        if pair * 2 * PACK >= key_count:
            break
        both = lax.dot_general(
            paired_queries,
            keys[key_count:, pair * 128 : (pair + 1) * 128],
            contract,
            preferred_element_type=jnp.float32,
        )
        parts += [both[:rows], both[rows:]]
    rotary = jnp.concatenate(parts, axis=1)[:, :key_count]
    scores = (scores + rotary) * score_scale
    row_steps = lax.rem(lax.broadcasted_iota(jnp.int32, (rows, 1), 0), miss_rows)
    key_steps = lax.broadcasted_iota(jnp.int32, (rows, key_count), 1)
    fresh_end = cached_rows + jnp.minimum(row_steps + 1, misses)
    allowed = (key_steps < hits * PAGE) | ((key_steps >= cached_rows) & (key_steps < fresh_end))
    scores = jnp.where(allowed, scores, -jnp.inf)
    row_max = jnp.max(scores, axis=1, keepdims=True)
    weights = jnp.exp(scores - row_max)
    total = jnp.sum(weights, axis=1, keepdims=True)
    context = jnp.dot(
        weights.astype(jnp.bfloat16), latent_keys, preferred_element_type=jnp.float32
    )
    return jnp.where(row_steps < misses, context / total, 0.0)


def attend_body(key_count, miss_rows, hits, misses, picks, lq, pq, keys, context, pages):
    prompt = pl.program_id(0)
    result = attend_one(
        lq[0], pq[0], keys.at[0], hits[prompt], misses[prompt], key_count, miss_rows
    ).astype(context.dtype)
    for head in range(result.shape[0] // miss_rows):
        context[:, head * LATENT_WIDTH : (head + 1) * LATENT_WIDTH] = result[
            head * miss_rows : (head + 1) * miss_rows
        ]
    slots = pages.shape[1]
    for rank in range(slots):
        page = picks[prompt * slots + rank]
        live = page >= 0
        page = jnp.maximum(page, 0)
        latent = keys[0, pl.ds(pl.multiple_of(page * PAGE, PAGE), PAGE), :]
        place = pl.multiple_of(key_count + lax.rem(page, PACK // PAGE) * PAGE, PAGE)
        packed = keys[0, pl.ds(place, PAGE), :]
        part = page // (PACK // PAGE)
        rotary = packed[:, :ROPE]
        for index in range(1, LATENT_WIDTH // ROPE):
            rotary = jnp.where(part == index, packed[:, index * ROPE : (index + 1) * ROPE], rotary)
        pages[0, rank, :, :LATENT_WIDTH] = jnp.where(live, latent, jnp.zeros_like(latent))
        pages[0, rank, :, LATENT_WIDTH:] = jnp.where(live, rotary, jnp.zeros_like(rotary))


def attend(latent_queries, paired_queries, keys, hits, misses, picks, key_count, miss_rows):
    prompts, rows, _ = latent_queries.shape
    heads = rows // miss_rows
    slots = picks.shape[1]
    whole = lambda shape: pl.BlockSpec((1,) + shape, lambda p, *_: (p,) + (0,) * len(shape))
    return pl.pallas_call(
        functools.partial(attend_body, key_count, miss_rows),
        grid_spec=pltpu.PrefetchScalarGridSpec(
            num_scalar_prefetch=3,
            grid=(prompts,),
            in_specs=[
                whole(latent_queries.shape[1:]),
                whole(paired_queries.shape[1:]),
                whole(keys.shape[1:]),
            ],
            out_specs=[
                pl.BlockSpec((miss_rows, heads * LATENT_WIDTH), lambda p, *_: (p, 0)),
                whole((slots, PAGE, LATENT_WIDTH + ROPE)),
            ],
        ),
        out_shape=[
            jax.ShapeDtypeStruct((prompts * miss_rows, heads * LATENT_WIDTH), jnp.bfloat16),
            jax.ShapeDtypeStruct((prompts, slots, PAGE, LATENT_WIDTH + ROPE), jnp.bfloat16),
        ],
        compiler_params=pltpu.CompilerParams(vmem_limit_bytes=40 * 1024 * 1024),
    )(hits, misses, picks.reshape(-1), latent_queries, paired_queries, keys)


def shards(
    queries,
    pool_cache,
    new_raw,
    norm_gain,
    hit_pages,
    prompt_len,
    page_holder,
    page_slot,
    page_owner,
):
    pool_size = lax.axis_size("pool")
    device_index = lax.axis_index("pool")
    pages_max = page_holder.shape[1]
    slot_cap = max(2, 2 * pages_max // pool_size)
    features = pool_cache.shape[1] // PAGE
    misses = prompt_len - PAGE * hit_pages
    page_steps = jnp.arange(pages_max)
    page_live = page_steps[None, :] < hit_pages[:, None]
    held_here = page_live & (page_holder == device_index)
    held_rank = jnp.cumsum(held_here.astype(jnp.int32), axis=1) - 1
    cap_steps = jnp.arange(slot_cap)
    chosen = held_here[:, None, :] & (held_rank[:, None, :] == cap_steps[None, :, None])
    slot_index = jnp.sum(jnp.where(chosen, page_slot[:, None, :], 0), axis=2).reshape(-1)
    filled = jnp.any(chosen, axis=2).reshape(-1, 1)
    outbox = jnp.where(filled, pool_cache[slot_index], jnp.zeros((), pool_cache.dtype))
    arrived = lax.all_to_all(outbox, "pool", split_axis=0, concat_axis=0, tiled=True)
    own_hit = hit_pages[device_index]
    own_miss = misses[device_index]
    own_holder = page_holder[device_index]
    own_owner = page_owner[device_index, :, 0]
    own_live = page_steps < own_hit
    before = (
        (page_steps[None, :] < page_steps[:, None])
        & (own_holder[None, :] == own_holder[:, None])
        & own_live[None, :]
    )
    page_rank = jnp.sum(before.astype(jnp.int32), axis=1)
    source = jnp.where(own_live, own_holder * slot_cap + page_rank, 0)
    cached_pages = arrived[source]
    new_rows = new_raw.shape[0] * PAGE
    new_keys = fresh_keys(
        new_raw.astype(jnp.float32).reshape(new_rows, features), norm_gain, own_hit, own_miss
    )
    new_pages = new_keys.reshape(-1, PAGE * features)
    per_prompt = new_pages.shape[0]
    total = pages_max + per_prompt
    push_cap = max(2, (total + pool_size - 1) // pool_size)
    slot_total = pool_size * push_cap
    new_steps = jnp.arange(per_prompt)
    own_keys = jnp.concatenate([cached_pages.reshape(pages_max * PAGE, features), new_keys], axis=0)
    member = device_index % TPW
    group_base = device_index - member
    group_hits = lax.dynamic_slice_in_dim(hit_pages, group_base, TPW)
    group_misses = lax.dynamic_slice_in_dim(misses, group_base, TPW)
    head_dev = queries.shape[2] // features
    query_rows = queries.reshape(TPW, -1, head_dev, features)
    miss_rows = query_rows.shape[1]
    latent_queries, paired_queries = turn_queries(query_rows, group_hits)
    keys = gather_keys(pack_keys(own_keys))
    group_owner = lax.dynamic_slice_in_dim(page_owner[:, :, 0], group_base, TPW)
    group_live = jnp.concatenate(
        [page_steps < group_hits[:, None], new_steps * PAGE < group_misses[:, None]], axis=1
    )
    taken = group_live & (group_owner == device_index)
    rank = jnp.cumsum(taken.astype(jnp.int32), axis=1) - 1
    all_steps = jnp.arange(total)
    hit = taken[:, None, :] & (rank[:, None, :] == jnp.arange(push_cap)[None, :, None])
    picks = jnp.sum(jnp.where(hit, all_steps + 1, 0), axis=2) - 1
    context, pages = attend(
        latent_queries,
        paired_queries,
        keys,
        group_hits,
        group_misses,
        picks,
        own_keys.shape[0],
        miss_rows,
    )
    if pool_size == TPW:
        delivered = pages.reshape(slot_total, PAGE * features)
    else:
        all_live = jnp.concatenate([own_live, new_steps * PAGE < own_miss], axis=0)
        same_owner = (
            (all_steps[None, :] < all_steps[:, None])
            & (own_owner[None, :] == own_owner[:, None])
            & all_live[None, :]
        )
        slot_position = own_owner * push_cap + jnp.sum(same_owner.astype(jnp.int32), axis=1)
        every_page = jnp.concatenate([cached_pages, new_pages], axis=0)
        outgoing = pick_rows(slot_position, all_live, every_page, slot_total)
        delivered = lax.all_to_all(outgoing, "pool", split_axis=0, concat_axis=0, tiled=True)
    return (context[None], delivered)


def solution(mesh):
    in_specs = (
        P(("groups", "pool"), None, None),
        P(("groups", "pool"), None),
        P(("groups", "pool"), None),
        P(),
        P("groups"),
        P("groups"),
        P("groups", None),
        P("groups", None),
        P("groups", None, None),
    )
    out_specs = (P(("groups", "pool"), None, None), P(("groups", "pool"), None))
    return jax.shard_map(shards, mesh=mesh, in_specs=in_specs, out_specs=out_specs, check_vma=False)
```

```python
import functools

import jax
import jax.numpy as jnp
from jax import lax
from jax.experimental import pallas as pl
from jax.experimental.pallas import tpu as pltpu
from jax.sharding import PartitionSpec as P

LATENT_WIDTH = 512
ROPE = 64
PAGE = 16
TPW = 16
PACK = 128
MESH = pl.DeviceIdType.MESH


score_scale = 0.07216878364870323
rope_base = 10000.0
norm_eps = 1e-06


def rope_tables(positions, rotary_width):
    half_width = rotary_width // 2
    frequencies = rope_base ** (jnp.arange(half_width).astype(jnp.float32) * (-2.0 / rotary_width))
    angles = positions.astype(jnp.float32)[:, None] * frequencies[None, :]
    return (jnp.cos(angles), jnp.sin(angles))


def rotate(values, cosine, sine_table):
    half_width = values.shape[-1] // 2
    lower = values[..., :half_width]
    upper = values[..., half_width:]
    return jnp.concatenate(
        [lower * cosine - upper * sine_table, upper * cosine + lower * sine_table], axis=-1
    )


def fresh_keys(raw_rows, norm_gain, hit_count, miss_count):
    latent = raw_rows[:, :LATENT_WIDTH]
    rotary = raw_rows[:, LATENT_WIDTH:]
    mean_square = jnp.mean(latent * latent, axis=1, keepdims=True)
    normed = latent * lax.rsqrt(mean_square + norm_eps) * norm_gain.astype(jnp.float32)[None, :]
    row_steps = jnp.arange(raw_rows.shape[0])
    cosine, sine_table = rope_tables(hit_count * PAGE + row_steps, ROPE)
    turned = rotate(rotary, cosine, sine_table)
    joined = jnp.concatenate([normed, turned], axis=1)
    return jnp.where((row_steps < miss_count)[:, None], joined, 0.0).astype(jnp.bfloat16)


def pick_rows(slot_position, valid_rows, rows, slot_total):
    selector = (jnp.arange(slot_total)[:, None] == slot_position[None, :]) & valid_rows[None, :]
    return jnp.dot(selector.astype(jnp.bfloat16), rows, preferred_element_type=jnp.float32).astype(
        jnp.bfloat16
    )


def turn_queries(query_rows, hits):
    batch, miss_rows = (query_rows.shape[0], query_rows.shape[1])
    row_steps = jnp.arange(miss_rows)
    positions = (hits[:, None] * PAGE + row_steps[None, :]).reshape(-1)
    cosine, sine_table = rope_tables(positions, ROPE)
    cosine = cosine.reshape(batch, miss_rows, 1, -1)
    sine_table = sine_table.reshape(batch, miss_rows, 1, -1)
    turned = rotate(query_rows[..., LATENT_WIDTH:].astype(jnp.float32), cosine, sine_table).astype(
        jnp.bfloat16
    )
    by_head = lambda value: value.transpose(0, 2, 1, 3).reshape(batch, -1, value.shape[-1])
    latent = by_head(query_rows[..., :LATENT_WIDTH])
    rotary = by_head(turned)
    blank = jnp.zeros_like(rotary)
    paired = jnp.concatenate(
        [jnp.concatenate([rotary, blank], axis=2), jnp.concatenate([blank, rotary], axis=2)], axis=1
    )
    return latent, paired


def pack_keys(keys):
    rotary = keys[:, LATENT_WIDTH:]
    spare = PACK * (LATENT_WIDTH // ROPE) - keys.shape[0]
    rotary = jnp.concatenate([rotary, jnp.zeros((spare, ROPE), keys.dtype)], axis=0)
    packed = rotary.reshape(-1, PACK, ROPE).transpose(1, 0, 2).reshape(PACK, LATENT_WIDTH)
    return jnp.concatenate([keys[:, :LATENT_WIDTH], packed], axis=0)


def attend_one(latent_queries, paired_queries, keys, hits, misses, key_count, miss_rows):
    rows = latent_queries.shape[0]
    cached_rows = key_count - miss_rows
    contract = (((1,), (1,)), ((), ()))
    latent_keys = keys[:key_count, :]
    scores = lax.dot_general(
        latent_queries, latent_keys, contract, preferred_element_type=jnp.float32
    )
    parts = []
    for pair in range(LATENT_WIDTH // 128):
        if pair * 2 * PACK >= key_count:
            break
        both = lax.dot_general(
            paired_queries,
            keys[key_count:, pair * 128 : (pair + 1) * 128],
            contract,
            preferred_element_type=jnp.float32,
        )
        parts += [both[:rows], both[rows:]]
    rotary = jnp.concatenate(parts, axis=1)[:, :key_count]
    scores = (scores + rotary) * score_scale
    row_steps = lax.rem(lax.broadcasted_iota(jnp.int32, (rows, 1), 0), miss_rows)
    key_steps = lax.broadcasted_iota(jnp.int32, (rows, key_count), 1)
    fresh_end = cached_rows + jnp.minimum(row_steps + 1, misses)
    allowed = (key_steps < hits * PAGE) | ((key_steps >= cached_rows) & (key_steps < fresh_end))
    scores = jnp.where(allowed, scores, -jnp.inf)
    row_max = jnp.max(scores, axis=1, keepdims=True)
    weights = jnp.exp(scores - row_max)
    total = jnp.sum(weights, axis=1, keepdims=True)
    context = jnp.dot(
        weights.astype(jnp.bfloat16), latent_keys, preferred_element_type=jnp.float32
    )
    return jnp.where(row_steps < misses, context / total, 0.0)


def serve_body(
    key_count, miss_rows, hits, misses, own, lq, pq, rows_sel, context, pages, keys, *sems
):
    local_sem, up_sem, down_sem, y_sem, core_sem, recv_sem = sems
    me = lax.axis_index("pool")
    member = lax.rem(me, TPW)
    base = me - member
    z, y, c = member // 4, lax.rem(member // 2, 2), lax.rem(member, 2)

    def slot_of(zz, yy, cc):
        return zz * 4 + yy * 2 + cc

    across = base + slot_of(z, 1 - y, c)
    twin = base + slot_of(z, y, 1 - c)
    above = base + slot_of(lax.rem(z + 1, 4), y, c)
    below = base + slot_of(lax.rem(z + 3, 4), y, c)
    has_up, has_down = z < 3, z > 0

    barrier = pltpu.get_barrier_semaphore()
    pl.semaphore_signal(barrier, inc=1, device_id={"pool": across}, device_id_type=MESH)
    pl.semaphore_signal(barrier, inc=1, device_id={"pool": twin}, device_id_type=MESH)

    @pl.when(has_up)
    def _():
        pl.semaphore_signal(barrier, inc=1, device_id={"pool": above}, device_id_type=MESH)

    @pl.when(has_down)
    def _():
        pl.semaphore_signal(barrier, inc=1, device_id={"pool": below}, device_id_type=MESH)

    mine = pltpu.make_async_copy(own, keys.at[member], local_sem)
    mine.start()
    pl.semaphore_wait(barrier, 2 + has_up.astype(jnp.int32) + has_down.astype(jnp.int32))
    mine.wait()

    def copy(zz, yy, cc, sem, device):
        slot = slot_of(zz, yy, cc)
        return pltpu.make_async_remote_copy(
            src_ref=keys.at[slot],
            dst_ref=keys.at[slot],
            send_sem=sem,
            recv_sem=recv_sem.at[slot],
            device_id={"pool": device},
            device_id_type=MESH,
        )

    def arrive(zz, yy, cc):
        copy(zz, yy, cc, core_sem.at[0], twin).wait_recv()

    def column(zz, act):
        @pl.when((zz <= z) & has_up)
        def _():
            act(copy(zz, y, c, up_sem.at[zz], above))

        @pl.when((zz >= z) & has_down)
        def _():
            act(copy(zz, y, c, down_sem.at[zz], below))

        act(copy(zz, y, c, y_sem.at[zz], across))
        act(copy(zz, y, c, core_sem.at[zz * 2 + y], twin))

    def work(slot):
        block = keys.at[slot]
        result = attend_one(
            lq[slot], pq[slot], block, hits[slot], misses[slot], key_count, miss_rows
        ).astype(context.dtype)
        place = pl.ds(pl.multiple_of(slot * miss_rows, miss_rows), miss_rows)
        for head in range(result.shape[0] // miss_rows):
            context[place, head * LATENT_WIDTH : (head + 1) * LATENT_WIDTH] = result[
                head * miss_rows : (head + 1) * miss_rows
            ]
        wide = -(-key_count // PACK) * PACK
        chosen = rows_sel[slot] == lax.broadcasted_iota(
            jnp.int32, (rows_sel.shape[1], wide), 1
        )
        chosen = chosen.astype(jnp.bfloat16)
        latent = jnp.dot(
            chosen[:, :key_count], block[:key_count, :], preferred_element_type=jnp.float32
        )
        sums = [jnp.zeros((rows_sel.shape[1], 128), jnp.float32)] * 2
        for chunk in range(wide // PACK):
            pair = chunk // 2
            sums[chunk % 2] += jnp.dot(
                chosen[:, chunk * PACK : (chunk + 1) * PACK],
                block[key_count:, pair * 128 : (pair + 1) * 128],
                preferred_element_type=jnp.float32,
            )
        rotary = sums[0][:, :ROPE] + sums[1][:, ROPE:]
        pages[slot, :, :LATENT_WIDTH] = latent.astype(pages.dtype)
        pages[slot, :, LATENT_WIDTH:] = rotary.astype(pages.dtype)

    def place_of(distance, way):
        zz = z + jnp.where(way == 0, -distance, distance)
        inside = (zz >= 0) & (zz <= 3) & (distance >= 0) & (distance <= 3)
        return jnp.clip(zz, 0, 3), inside & ((distance > 0) | (way == 0))

    def step(distance, carry):
        for way in range(2):
            zz, inside = place_of(distance, way)

            @pl.when(inside)
            def _():
                @pl.when(distance > 0)
                def _():
                    arrive(zz, y, c)

                column(zz, lambda item: item.start())

        for way in range(2):
            zz, inside = place_of(distance - 1, way)

            @pl.when(inside)
            def _():
                arrive(zz, 1 - y, c)
                copy(zz, 1 - y, c, core_sem.at[zz * 2 + 1 - y], twin).start()

        def one(index, carry):
            way = lax.rem(index, 2)
            cc = lax.rem(c + lax.rem(index // 2, 2), 2)
            side = index // 4
            yy = lax.rem(y + side, 2)
            zz, inside = place_of(distance - side, way)

            @pl.when(inside)
            def _():
                @pl.when(cc != c)
                def _():
                    arrive(zz, yy, cc)

                work(slot_of(zz, yy, cc))

            return carry

        return lax.fori_loop(0, 8, one, carry)

    lax.fori_loop(0, 5, step, 0)

    def finish(zz, carry):
        column(zz, lambda item: item.wait_send())
        copy(zz, 1 - y, c, core_sem.at[zz * 2 + 1 - y], twin).wait_send()
        return carry

    lax.fori_loop(0, 4, finish, 0)


def serve(own, latent_queries, paired_queries, hits, misses, picks, key_count, miss_rows):
    prompts, rows, _ = latent_queries.shape
    heads = rows // miss_rows
    picked = picks[:, :, None] * PAGE + jnp.arange(PAGE)
    picked = jnp.where(picks[:, :, None] >= 0, picked, -1).reshape(prompts, -1, 1)
    vmem = pl.BlockSpec(memory_space=pltpu.VMEM)
    smem = pl.BlockSpec(memory_space=pltpu.SMEM)
    return pl.pallas_call(
        functools.partial(serve_body, key_count, miss_rows),
        out_shape=[
            jax.ShapeDtypeStruct((prompts * miss_rows, heads * LATENT_WIDTH), jnp.bfloat16),
            jax.ShapeDtypeStruct((prompts, picked.shape[1], LATENT_WIDTH + ROPE), jnp.bfloat16),
        ],
        in_specs=[smem, smem, vmem, vmem, vmem, vmem],
        out_specs=[vmem, vmem],
        scratch_shapes=[
            pltpu.VMEM((TPW,) + own.shape, own.dtype),
            pltpu.SemaphoreType.DMA,
            pltpu.SemaphoreType.DMA((4,)),
            pltpu.SemaphoreType.DMA((4,)),
            pltpu.SemaphoreType.DMA((4,)),
            pltpu.SemaphoreType.DMA((8,)),
            pltpu.SemaphoreType.DMA((TPW,)),
        ],
        compiler_params=pltpu.CompilerParams(
            collective_id=0, has_side_effects=True, vmem_limit_bytes=48 * 1024 * 1024
        ),
    )(hits, misses, own, latent_queries, paired_queries, picked)


def shards(
    queries,
    pool_cache,
    new_raw,
    norm_gain,
    hit_pages,
    prompt_len,
    page_holder,
    page_slot,
    page_owner,
):
    pool_size = lax.axis_size("pool")
    device_index = lax.axis_index("pool")
    pages_max = page_holder.shape[1]
    slot_cap = max(2, 2 * pages_max // pool_size)
    features = pool_cache.shape[1] // PAGE
    misses = prompt_len - PAGE * hit_pages
    page_steps = jnp.arange(pages_max)
    page_live = page_steps[None, :] < hit_pages[:, None]
    held_here = page_live & (page_holder == device_index)
    held_rank = jnp.cumsum(held_here.astype(jnp.int32), axis=1) - 1
    cap_steps = jnp.arange(slot_cap)
    chosen = held_here[:, None, :] & (held_rank[:, None, :] == cap_steps[None, :, None])
    slot_index = jnp.sum(jnp.where(chosen, page_slot[:, None, :], 0), axis=2).reshape(-1)
    filled = jnp.any(chosen, axis=2).reshape(-1, 1)
    outbox = jnp.where(filled, pool_cache[slot_index], jnp.zeros((), pool_cache.dtype))
    arrived = lax.all_to_all(outbox, "pool", split_axis=0, concat_axis=0, tiled=True)
    own_hit = hit_pages[device_index]
    own_miss = misses[device_index]
    own_holder = page_holder[device_index]
    own_owner = page_owner[device_index, :, 0]
    own_live = page_steps < own_hit
    before = (
        (page_steps[None, :] < page_steps[:, None])
        & (own_holder[None, :] == own_holder[:, None])
        & own_live[None, :]
    )
    page_rank = jnp.sum(before.astype(jnp.int32), axis=1)
    source = jnp.where(own_live, own_holder * slot_cap + page_rank, 0)
    cached_pages = arrived[source]
    new_rows = new_raw.shape[0] * PAGE
    new_keys = fresh_keys(
        new_raw.astype(jnp.float32).reshape(new_rows, features), norm_gain, own_hit, own_miss
    )
    new_pages = new_keys.reshape(-1, PAGE * features)
    per_prompt = new_pages.shape[0]
    total = pages_max + per_prompt
    push_cap = max(2, (total + pool_size - 1) // pool_size)
    slot_total = pool_size * push_cap
    new_steps = jnp.arange(per_prompt)
    own_keys = jnp.concatenate([cached_pages.reshape(pages_max * PAGE, features), new_keys], axis=0)
    member = device_index % TPW
    group_base = device_index - member
    group_hits = lax.dynamic_slice_in_dim(hit_pages, group_base, TPW)
    group_misses = lax.dynamic_slice_in_dim(misses, group_base, TPW)
    head_dev = queries.shape[2] // features
    query_rows = queries.reshape(TPW, -1, head_dev, features)
    miss_rows = query_rows.shape[1]
    latent_queries, paired_queries = turn_queries(query_rows, group_hits)
    group_owner = lax.dynamic_slice_in_dim(page_owner[:, :, 0], group_base, TPW)
    group_live = jnp.concatenate(
        [page_steps < group_hits[:, None], new_steps * PAGE < group_misses[:, None]], axis=1
    )
    taken = group_live & (group_owner == device_index)
    rank = jnp.cumsum(taken.astype(jnp.int32), axis=1) - 1
    all_steps = jnp.arange(total)
    hit = taken[:, None, :] & (rank[:, None, :] == jnp.arange(push_cap)[None, :, None])
    picks = jnp.sum(jnp.where(hit, all_steps + 1, 0), axis=2) - 1
    context, pages = serve(
        pack_keys(own_keys),
        latent_queries,
        paired_queries,
        group_hits,
        group_misses,
        picks,
        own_keys.shape[0],
        miss_rows,
    )
    if pool_size == TPW:
        delivered = pages.reshape(slot_total, PAGE * features)
    else:
        all_live = jnp.concatenate([own_live, new_steps * PAGE < own_miss], axis=0)
        same_owner = (
            (all_steps[None, :] < all_steps[:, None])
            & (own_owner[None, :] == own_owner[:, None])
            & all_live[None, :]
        )
        slot_position = own_owner * push_cap + jnp.sum(same_owner.astype(jnp.int32), axis=1)
        every_page = jnp.concatenate([cached_pages, new_pages], axis=0)
        outgoing = pick_rows(slot_position, all_live, every_page, slot_total)
        delivered = lax.all_to_all(outgoing, "pool", split_axis=0, concat_axis=0, tiled=True)
    return (context[None], delivered)


def solution(mesh):
    in_specs = (
        P(("groups", "pool"), None, None),
        P(("groups", "pool"), None),
        P(("groups", "pool"), None),
        P(),
        P("groups"),
        P("groups"),
        P("groups", None),
        P("groups", None),
        P("groups", None, None),
    )
    out_specs = (P(("groups", "pool"), None, None), P(("groups", "pool"), None))
    return jax.shard_map(shards, mesh=mesh, in_specs=in_specs, out_specs=out_specs, check_vma=False)
```

```python
import functools

import jax
import jax.numpy as jnp
from jax import lax
from jax.experimental import pallas as pl
from jax.experimental.pallas import tpu as pltpu
from jax.sharding import PartitionSpec as P

LATENT_WIDTH = 512
ROPE = 64
PAGE = 16
TPW = 16
PACK = 128
MESH = pl.DeviceIdType.MESH


score_scale = 0.07216878364870323
rope_base = 10000.0
norm_eps = 1e-06


def rope_tables(positions, rotary_width):
    half_width = rotary_width // 2
    frequencies = rope_base ** (jnp.arange(half_width).astype(jnp.float32) * (-2.0 / rotary_width))
    angles = positions.astype(jnp.float32)[:, None] * frequencies[None, :]
    return (jnp.cos(angles), jnp.sin(angles))


def rotate(values, cosine, sine_table):
    half_width = values.shape[-1] // 2
    lower = values[..., :half_width]
    upper = values[..., half_width:]
    return jnp.concatenate(
        [lower * cosine - upper * sine_table, upper * cosine + lower * sine_table], axis=-1
    )


def fresh_keys(raw_rows, norm_gain, hit_count, miss_count):
    latent = raw_rows[:, :LATENT_WIDTH]
    rotary = raw_rows[:, LATENT_WIDTH:]
    mean_square = jnp.mean(latent * latent, axis=1, keepdims=True)
    normed = latent * lax.rsqrt(mean_square + norm_eps) * norm_gain.astype(jnp.float32)[None, :]
    row_steps = jnp.arange(raw_rows.shape[0])
    cosine, sine_table = rope_tables(hit_count * PAGE + row_steps, ROPE)
    turned = rotate(rotary, cosine, sine_table)
    joined = jnp.concatenate([normed, turned], axis=1)
    return jnp.where((row_steps < miss_count)[:, None], joined, 0.0).astype(jnp.bfloat16)


def pick_rows(slot_position, valid_rows, rows, slot_total):
    selector = (jnp.arange(slot_total)[:, None] == slot_position[None, :]) & valid_rows[None, :]
    return jnp.dot(selector.astype(jnp.bfloat16), rows, preferred_element_type=jnp.float32).astype(
        jnp.bfloat16
    )


def turn_queries(query_rows, hits):
    batch, miss_rows = (query_rows.shape[0], query_rows.shape[1])
    row_steps = jnp.arange(miss_rows)
    positions = (hits[:, None] * PAGE + row_steps[None, :]).reshape(-1)
    cosine, sine_table = rope_tables(positions, ROPE)
    cosine = cosine.reshape(batch, miss_rows, 1, -1)
    sine_table = sine_table.reshape(batch, miss_rows, 1, -1)
    turned = rotate(query_rows[..., LATENT_WIDTH:].astype(jnp.float32), cosine, sine_table).astype(
        jnp.bfloat16
    )
    by_head = lambda value: value.transpose(0, 2, 1, 3).reshape(batch, -1, value.shape[-1])
    latent = by_head(query_rows[..., :LATENT_WIDTH])
    rotary = by_head(turned)
    blank = jnp.zeros_like(rotary)
    paired = jnp.concatenate(
        [jnp.concatenate([rotary, blank], axis=2), jnp.concatenate([blank, rotary], axis=2)], axis=1
    )
    return latent, paired


def pack_keys(keys):
    rotary = keys[:, LATENT_WIDTH:]
    spare = PACK * (LATENT_WIDTH // ROPE) - keys.shape[0]
    rotary = jnp.concatenate([rotary, jnp.zeros((spare, ROPE), keys.dtype)], axis=0)
    packed = rotary.reshape(-1, PACK, ROPE).transpose(1, 0, 2).reshape(PACK, LATENT_WIDTH)
    return jnp.concatenate([keys[:, :LATENT_WIDTH], packed], axis=0)


def attend_one(latent_queries, paired_queries, keys, hits, misses, key_count, miss_rows):
    rows = latent_queries.shape[0]
    cached_rows = key_count - miss_rows
    contract = (((1,), (1,)), ((), ()))
    latent_keys = keys[:key_count, :]
    scores = lax.dot_general(
        latent_queries, latent_keys, contract, preferred_element_type=jnp.float32
    )
    parts = []
    for pair in range(LATENT_WIDTH // 128):
        if pair * 2 * PACK >= key_count:
            break
        both = lax.dot_general(
            paired_queries,
            keys[key_count:, pair * 128 : (pair + 1) * 128],
            contract,
            preferred_element_type=jnp.float32,
        )
        parts += [both[:rows], both[rows:]]
    rotary = jnp.concatenate(parts, axis=1)[:, :key_count]
    scores = (scores + rotary) * score_scale
    row_steps = lax.rem(lax.broadcasted_iota(jnp.int32, (rows, 1), 0), miss_rows)
    key_steps = lax.broadcasted_iota(jnp.int32, (rows, key_count), 1)
    fresh_end = cached_rows + jnp.minimum(row_steps + 1, misses)
    allowed = (key_steps < hits * PAGE) | ((key_steps >= cached_rows) & (key_steps < fresh_end))
    scores = jnp.where(allowed, scores, -jnp.inf)
    row_max = jnp.max(scores, axis=1, keepdims=True)
    weights = jnp.exp(scores - row_max)
    total = jnp.sum(weights, axis=1, keepdims=True)
    context = jnp.dot(
        weights.astype(jnp.bfloat16), latent_keys, preferred_element_type=jnp.float32
    )
    return jnp.where(row_steps < misses, context / total, 0.0)


def serve_body(
    key_count, miss_rows, hits, misses, own, lq, pq, rows_sel, context, pages, keys, *sems
):
    local_sem, up_sem, down_sem, y_sem, core_sem, extra_sem, half_sem, recv_sem = sems
    me = lax.axis_index("pool")
    member = lax.rem(me, TPW)
    base = me - member
    z, y, c = member // 4, lax.rem(member // 2, 2), lax.rem(member, 2)

    def slot_of(zz, yy, cc):
        return zz * 4 + yy * 2 + cc

    across = base + slot_of(z, 1 - y, c)
    twin = base + slot_of(z, y, 1 - c)
    above = base + slot_of(lax.rem(z + 1, 4), y, c)
    below = base + slot_of(lax.rem(z + 3, 4), y, c)
    has_up, has_down = z < 3, z > 0
    edge_z = jnp.where(z < 2, 0, 3)
    far_z = 3 - edge_z
    edge = z == edge_z
    middle = z != edge_z
    mate = base + slot_of(z + 1 - 2 * lax.rem(z, 2), y, c)
    half_rows = own.shape[0] // 2

    barrier = pltpu.get_barrier_semaphore()
    pl.semaphore_signal(barrier, inc=1, device_id={"pool": across}, device_id_type=MESH)
    pl.semaphore_signal(barrier, inc=1, device_id={"pool": twin}, device_id_type=MESH)

    @pl.when(has_up)
    def _():
        pl.semaphore_signal(barrier, inc=1, device_id={"pool": above}, device_id_type=MESH)

    @pl.when(has_down)
    def _():
        pl.semaphore_signal(barrier, inc=1, device_id={"pool": below}, device_id_type=MESH)

    mine = pltpu.make_async_copy(own, keys.at[member], local_sem)
    mine.start()
    pl.semaphore_wait(barrier, 2 + has_up.astype(jnp.int32) + has_down.astype(jnp.int32))
    mine.wait()

    def copy(zz, yy, cc, sem, device):
        slot = slot_of(zz, yy, cc)
        return pltpu.make_async_remote_copy(
            src_ref=keys.at[slot],
            dst_ref=keys.at[slot],
            send_sem=sem,
            recv_sem=recv_sem.at[slot],
            device_id={"pool": device},
            device_id_type=MESH,
        )

    def half_copy(zz, part, sem, arrived_sem, device, yy):
        piece = keys.at[slot_of(zz, yy, c), pl.ds(part * half_rows, half_rows)]
        return pltpu.make_async_remote_copy(
            src_ref=piece,
            dst_ref=piece,
            send_sem=sem,
            recv_sem=arrived_sem,
            device_id={"pool": device},
            device_id_type=MESH,
        )

    def arrive(zz, yy, cc):
        copy(zz, yy, cc, core_sem.at[0], twin).wait_recv()

    def column(zz, act):
        @pl.when((zz <= z) & has_up)
        def _():
            act(copy(zz, y, c, up_sem.at[zz], above))

        @pl.when((zz >= z) & has_down)
        def _():
            act(copy(zz, y, c, down_sem.at[zz], below))

        @pl.when((edge & (zz != far_z)) | (middle & (zz != edge_z)))
        def _():
            act(copy(zz, y, c, y_sem.at[zz], across))

        @pl.when(edge & (zz == far_z))
        def _():
            slot = slot_of(zz, y, c)
            act(half_copy(zz, 0, y_sem.at[zz], recv_sem.at[slot], across, y))

        act(copy(zz, y, c, core_sem.at[zz * 2 + y], twin))

    def extra(zz, act):
        @pl.when(edge & (zz == edge_z))
        def _():
            act(copy(zz, 1 - y, c, extra_sem, mate))

        @pl.when(middle & (zz == far_z))
        def _():
            act(half_copy(zz, 1, extra_sem, half_sem, mate, 1 - y))

    def arrive_side(zz):
        @pl.when((zz != far_z) | middle)
        def _():
            arrive(zz, 1 - y, c)

        @pl.when(edge & (zz == far_z))
        def _():
            slot = slot_of(zz, 1 - y, c)
            half_copy(zz, 0, extra_sem, recv_sem.at[slot], mate, 1 - y).wait_recv()
            half_copy(zz, 1, extra_sem, half_sem, mate, 1 - y).wait_recv()

    def work(slot):
        block = keys.at[slot]
        result = attend_one(
            lq[slot], pq[slot], block, hits[slot], misses[slot], key_count, miss_rows
        ).astype(context.dtype)
        place = pl.ds(pl.multiple_of(slot * miss_rows, miss_rows), miss_rows)
        for head in range(result.shape[0] // miss_rows):
            context[place, head * LATENT_WIDTH : (head + 1) * LATENT_WIDTH] = result[
                head * miss_rows : (head + 1) * miss_rows
            ]
        wide = -(-key_count // PACK) * PACK
        chosen = rows_sel[slot] == lax.broadcasted_iota(
            jnp.int32, (rows_sel.shape[1], wide), 1
        )
        chosen = chosen.astype(jnp.bfloat16)
        latent = jnp.dot(
            chosen[:, :key_count], block[:key_count, :], preferred_element_type=jnp.float32
        )
        sums = [jnp.zeros((rows_sel.shape[1], 128), jnp.float32)] * 2
        for chunk in range(wide // PACK):
            pair = chunk // 2
            sums[chunk % 2] += jnp.dot(
                chosen[:, chunk * PACK : (chunk + 1) * PACK],
                block[key_count:, pair * 128 : (pair + 1) * 128],
                preferred_element_type=jnp.float32,
            )
        rotary = sums[0][:, :ROPE] + sums[1][:, ROPE:]
        pages[slot, :, :LATENT_WIDTH] = latent.astype(pages.dtype)
        pages[slot, :, LATENT_WIDTH:] = rotary.astype(pages.dtype)

    def place_of(distance, way):
        zz = z + jnp.where(way == 0, -distance, distance)
        inside = (zz >= 0) & (zz <= 3) & (distance >= 0) & (distance <= 3)
        return jnp.clip(zz, 0, 3), inside & ((distance > 0) | (way == 0))

    def step(distance, carry):
        for way in range(2):
            zz, inside = place_of(distance, way)

            @pl.when(inside)
            def _():
                @pl.when(distance > 0)
                def _():
                    arrive(zz, y, c)

                column(zz, lambda item: item.start())

        for way in range(2):
            zz, inside = place_of(distance - 1, way)

            @pl.when(inside)
            def _():
                arrive_side(zz)
                extra(zz, lambda item: item.start())
                copy(zz, 1 - y, c, core_sem.at[zz * 2 + 1 - y], twin).start()

        def one(index, carry):
            way = lax.rem(index, 2)
            cc = lax.rem(c + lax.rem(index // 2, 2), 2)
            side = index // 4
            yy = lax.rem(y + side, 2)
            zz, inside = place_of(distance - side, way)

            @pl.when(inside)
            def _():
                @pl.when(cc != c)
                def _():
                    arrive(zz, yy, cc)

                work(slot_of(zz, yy, cc))

            return carry

        return lax.fori_loop(0, 8, one, carry)

    lax.fori_loop(0, 5, step, 0)

    def finish(zz, carry):
        column(zz, lambda item: item.wait_send())
        extra(zz, lambda item: item.wait_send())
        copy(zz, 1 - y, c, core_sem.at[zz * 2 + 1 - y], twin).wait_send()
        return carry

    lax.fori_loop(0, 4, finish, 0)


def serve(own, latent_queries, paired_queries, hits, misses, picks, key_count, miss_rows):
    prompts, rows, _ = latent_queries.shape
    heads = rows // miss_rows
    picked = picks[:, :, None] * PAGE + jnp.arange(PAGE)
    picked = jnp.where(picks[:, :, None] >= 0, picked, -1).reshape(prompts, -1, 1)
    vmem = pl.BlockSpec(memory_space=pltpu.VMEM)
    smem = pl.BlockSpec(memory_space=pltpu.SMEM)
    return pl.pallas_call(
        functools.partial(serve_body, key_count, miss_rows),
        out_shape=[
            jax.ShapeDtypeStruct((prompts * miss_rows, heads * LATENT_WIDTH), jnp.bfloat16),
            jax.ShapeDtypeStruct((prompts, picked.shape[1], LATENT_WIDTH + ROPE), jnp.bfloat16),
        ],
        in_specs=[smem, smem, vmem, vmem, vmem, vmem],
        out_specs=[vmem, vmem],
        scratch_shapes=[
            pltpu.VMEM((TPW,) + own.shape, own.dtype),
            pltpu.SemaphoreType.DMA,
            pltpu.SemaphoreType.DMA((4,)),
            pltpu.SemaphoreType.DMA((4,)),
            pltpu.SemaphoreType.DMA((4,)),
            pltpu.SemaphoreType.DMA((8,)),
            pltpu.SemaphoreType.DMA,
            pltpu.SemaphoreType.DMA,
            pltpu.SemaphoreType.DMA((TPW,)),
        ],
        compiler_params=pltpu.CompilerParams(
            collective_id=0, has_side_effects=True, vmem_limit_bytes=36 * 1024 * 1024
        ),
    )(hits, misses, own, latent_queries, paired_queries, picked)


def shards(
    queries,
    pool_cache,
    new_raw,
    norm_gain,
    hit_pages,
    prompt_len,
    page_holder,
    page_slot,
    page_owner,
):
    pool_size = lax.axis_size("pool")
    device_index = lax.axis_index("pool")
    pages_max = page_holder.shape[1]
    slot_cap = max(2, 2 * pages_max // pool_size)
    features = pool_cache.shape[1] // PAGE
    misses = prompt_len - PAGE * hit_pages
    page_steps = jnp.arange(pages_max)
    page_live = page_steps[None, :] < hit_pages[:, None]
    held_here = page_live & (page_holder == device_index)
    held_rank = jnp.cumsum(held_here.astype(jnp.int32), axis=1) - 1
    cap_steps = jnp.arange(slot_cap)
    chosen = held_here[:, None, :] & (held_rank[:, None, :] == cap_steps[None, :, None])
    slot_index = jnp.sum(jnp.where(chosen, page_slot[:, None, :], 0), axis=2).reshape(-1)
    outbox = pool_cache[slot_index]
    arrived = lax.all_to_all(outbox, "pool", split_axis=0, concat_axis=0, tiled=True)
    own_hit = hit_pages[device_index]
    own_miss = misses[device_index]
    own_holder = page_holder[device_index]
    own_owner = page_owner[device_index, :, 0]
    own_live = page_steps < own_hit
    before = (
        (page_steps[None, :] < page_steps[:, None])
        & (own_holder[None, :] == own_holder[:, None])
        & own_live[None, :]
    )
    page_rank = jnp.sum(before.astype(jnp.int32), axis=1)
    source = jnp.where(own_live, own_holder * slot_cap + page_rank, 0)
    cached_pages = arrived[source]
    new_rows = new_raw.shape[0] * PAGE
    new_keys = fresh_keys(
        new_raw.astype(jnp.float32).reshape(new_rows, features), norm_gain, own_hit, own_miss
    )
    new_pages = new_keys.reshape(-1, PAGE * features)
    per_prompt = new_pages.shape[0]
    total = pages_max + per_prompt
    push_cap = max(2, (total + pool_size - 1) // pool_size)
    slot_total = pool_size * push_cap
    new_steps = jnp.arange(per_prompt)
    own_keys = jnp.concatenate([cached_pages.reshape(pages_max * PAGE, features), new_keys], axis=0)
    member = device_index % TPW
    group_base = device_index - member
    group_hits = lax.dynamic_slice_in_dim(hit_pages, group_base, TPW)
    group_misses = lax.dynamic_slice_in_dim(misses, group_base, TPW)
    head_dev = queries.shape[2] // features
    query_rows = queries.reshape(TPW, -1, head_dev, features)
    miss_rows = query_rows.shape[1]
    latent_queries, paired_queries = turn_queries(query_rows, group_hits)
    group_owner = lax.dynamic_slice_in_dim(page_owner[:, :, 0], group_base, TPW)
    group_live = jnp.concatenate(
        [page_steps < group_hits[:, None], new_steps * PAGE < group_misses[:, None]], axis=1
    )
    taken = group_live & (group_owner == device_index)
    rank = jnp.cumsum(taken.astype(jnp.int32), axis=1) - 1
    all_steps = jnp.arange(total)
    hit = taken[:, None, :] & (rank[:, None, :] == jnp.arange(push_cap)[None, :, None])
    picks = jnp.sum(jnp.where(hit, all_steps + 1, 0), axis=2) - 1
    context, pages = serve(
        pack_keys(own_keys),
        latent_queries,
        paired_queries,
        group_hits,
        group_misses,
        picks,
        own_keys.shape[0],
        miss_rows,
    )
    if pool_size == TPW:
        delivered = pages.reshape(slot_total, PAGE * features)
    else:
        all_live = jnp.concatenate([own_live, new_steps * PAGE < own_miss], axis=0)
        same_owner = (
            (all_steps[None, :] < all_steps[:, None])
            & (own_owner[None, :] == own_owner[:, None])
            & all_live[None, :]
        )
        slot_position = own_owner * push_cap + jnp.sum(same_owner.astype(jnp.int32), axis=1)
        every_page = jnp.concatenate([cached_pages, new_pages], axis=0)
        outgoing = pick_rows(slot_position, all_live, every_page, slot_total)
        delivered = lax.all_to_all(outgoing, "pool", split_axis=0, concat_axis=0, tiled=True)
    return (context[None], delivered)


def solution(mesh):
    in_specs = (
        P(("groups", "pool"), None, None),
        P(("groups", "pool"), None),
        P(("groups", "pool"), None),
        P(),
        P("groups"),
        P("groups"),
        P("groups", None),
        P("groups", None),
        P("groups", None, None),
    )
    out_specs = (P(("groups", "pool"), None, None), P(("groups", "pool"), None))
    return jax.shard_map(shards, mesh=mesh, in_specs=in_specs, out_specs=out_specs, check_vma=False)
```

```python
import functools

import jax
import jax.numpy as jnp
from jax import lax
from jax.experimental import pallas as pl
from jax.experimental.pallas import tpu as pltpu
from jax.sharding import PartitionSpec as P

LATENT_WIDTH = 512
ROPE = 64
PAGE = 16
TPW = 16
PACK = 128
MESH = pl.DeviceIdType.MESH


score_scale = 0.07216878364870323
rope_base = 10000.0
norm_eps = 1e-06


def rope_tables(positions, rotary_width):
    half_width = rotary_width // 2
    frequencies = rope_base ** (jnp.arange(half_width).astype(jnp.float32) * (-2.0 / rotary_width))
    angles = positions.astype(jnp.float32)[:, None] * frequencies[None, :]
    return (jnp.cos(angles), jnp.sin(angles))


def rotate(values, cosine, sine_table):
    half_width = values.shape[-1] // 2
    lower = values[..., :half_width]
    upper = values[..., half_width:]
    return jnp.concatenate(
        [lower * cosine - upper * sine_table, upper * cosine + lower * sine_table], axis=-1
    )


def fresh_keys(raw_rows, norm_gain, hit_count, miss_count):
    latent = raw_rows[:, :LATENT_WIDTH]
    rotary = raw_rows[:, LATENT_WIDTH:]
    mean_square = jnp.mean(latent * latent, axis=1, keepdims=True)
    normed = latent * lax.rsqrt(mean_square + norm_eps) * norm_gain.astype(jnp.float32)[None, :]
    row_steps = jnp.arange(raw_rows.shape[0])
    cosine, sine_table = rope_tables(hit_count * PAGE + row_steps, ROPE)
    turned = rotate(rotary, cosine, sine_table)
    joined = jnp.concatenate([normed, turned], axis=1)
    return jnp.where((row_steps < miss_count)[:, None], joined, 0.0).astype(jnp.bfloat16)


def pick_rows(slot_position, valid_rows, rows, slot_total):
    selector = (jnp.arange(slot_total)[:, None] == slot_position[None, :]) & valid_rows[None, :]
    return jnp.dot(selector.astype(jnp.bfloat16), rows, preferred_element_type=jnp.float32).astype(
        jnp.bfloat16
    )


def turn_queries(query_rows, hits):
    batch, miss_rows = (query_rows.shape[0], query_rows.shape[1])
    row_steps = jnp.arange(miss_rows)
    positions = (hits[:, None] * PAGE + row_steps[None, :]).reshape(-1)
    cosine, sine_table = rope_tables(positions, ROPE)
    cosine = cosine.reshape(batch, miss_rows, 1, -1)
    sine_table = sine_table.reshape(batch, miss_rows, 1, -1)
    turned = rotate(query_rows[..., LATENT_WIDTH:].astype(jnp.float32), cosine, sine_table).astype(
        jnp.bfloat16
    )
    by_head = lambda value: value.transpose(0, 2, 1, 3).reshape(batch, -1, value.shape[-1])
    latent = by_head(query_rows[..., :LATENT_WIDTH])
    rotary = by_head(turned)
    blank = jnp.zeros_like(rotary)
    paired = jnp.concatenate(
        [jnp.concatenate([rotary, blank], axis=2), jnp.concatenate([blank, rotary], axis=2)], axis=1
    )
    return latent, paired


def pack_keys(keys):
    rotary = keys[:, LATENT_WIDTH:]
    spare = PACK * (LATENT_WIDTH // ROPE) - keys.shape[0]
    rotary = jnp.concatenate([rotary, jnp.zeros((spare, ROPE), keys.dtype)], axis=0)
    packed = rotary.reshape(-1, PACK, ROPE).transpose(1, 0, 2).reshape(PACK, LATENT_WIDTH)
    return jnp.concatenate([keys[:, :LATENT_WIDTH], packed], axis=0)


def attend_one(latent_queries, paired_queries, keys, hits, misses, key_count, miss_rows):
    rows = latent_queries.shape[0]
    cached_rows = key_count - miss_rows
    contract = (((1,), (1,)), ((), ()))
    latent_keys = keys[:key_count, :]
    scores = lax.dot_general(
        latent_queries, latent_keys, contract, preferred_element_type=jnp.float32
    )
    parts = []
    for pair in range(LATENT_WIDTH // 128):
        if pair * 2 * PACK >= key_count:
            break
        both = lax.dot_general(
            paired_queries,
            keys[key_count:, pair * 128 : (pair + 1) * 128],
            contract,
            preferred_element_type=jnp.float32,
        )
        parts += [both[:rows], both[rows:]]
    rotary = jnp.concatenate(parts, axis=1)[:, :key_count]
    scores = (scores + rotary) * score_scale
    row_steps = lax.rem(lax.broadcasted_iota(jnp.int32, (rows, 1), 0), miss_rows)
    key_steps = lax.broadcasted_iota(jnp.int32, (rows, key_count), 1)
    fresh_end = cached_rows + jnp.minimum(row_steps + 1, misses)
    allowed = (key_steps < hits * PAGE) | ((key_steps >= cached_rows) & (key_steps < fresh_end))
    scores = jnp.where(allowed, scores, -jnp.inf)
    row_max = jnp.max(scores, axis=1, keepdims=True)
    weights = jnp.exp(scores - row_max)
    total = jnp.sum(weights, axis=1, keepdims=True)
    context = jnp.dot(
        weights.astype(jnp.bfloat16), latent_keys, preferred_element_type=jnp.float32
    )
    return jnp.where(row_steps < misses, context / total, 0.0)


def serve_body(
    key_count, miss_rows, hits, misses, own, lq, pq, rows_sel, context, pages, keys, *scratch
):
    lq_now, pq_now, context_now, lq_sem, pq_sem, context_sem = scratch[:6]
    local_sem, up_sem, down_sem, y_sem, core_sem, extra_sem, half_sem, recv_sem = scratch[6:]
    me = lax.axis_index("pool")
    member = lax.rem(me, TPW)
    base = me - member
    z, y, c = member // 4, lax.rem(member // 2, 2), lax.rem(member, 2)

    def slot_of(zz, yy, cc):
        return zz * 4 + yy * 2 + cc

    across = base + slot_of(z, 1 - y, c)
    twin = base + slot_of(z, y, 1 - c)
    above = base + slot_of(lax.rem(z + 1, 4), y, c)
    below = base + slot_of(lax.rem(z + 3, 4), y, c)
    has_up, has_down = z < 3, z > 0
    edge_z = jnp.where(z < 2, 0, 3)
    far_z = 3 - edge_z
    edge = z == edge_z
    middle = z != edge_z
    mate = base + slot_of(z + 1 - 2 * lax.rem(z, 2), y, c)
    half_rows = own.shape[0] // 2

    barrier = pltpu.get_barrier_semaphore()
    pl.semaphore_signal(barrier, inc=1, device_id={"pool": across}, device_id_type=MESH)
    pl.semaphore_signal(barrier, inc=1, device_id={"pool": twin}, device_id_type=MESH)

    @pl.when(has_up)
    def _():
        pl.semaphore_signal(barrier, inc=1, device_id={"pool": above}, device_id_type=MESH)

    @pl.when(has_down)
    def _():
        pl.semaphore_signal(barrier, inc=1, device_id={"pool": below}, device_id_type=MESH)

    mine = pltpu.make_async_copy(own, keys.at[member], local_sem)
    mine.start()
    pl.semaphore_wait(barrier, 2 + has_up.astype(jnp.int32) + has_down.astype(jnp.int32))
    mine.wait()

    def copy(zz, yy, cc, sem, device):
        slot = slot_of(zz, yy, cc)
        return pltpu.make_async_remote_copy(
            src_ref=keys.at[slot],
            dst_ref=keys.at[slot],
            send_sem=sem,
            recv_sem=recv_sem.at[slot],
            device_id={"pool": device},
            device_id_type=MESH,
        )

    def half_copy(zz, part, sem, arrived_sem, device, yy):
        piece = keys.at[slot_of(zz, yy, c), pl.ds(part * half_rows, half_rows)]
        return pltpu.make_async_remote_copy(
            src_ref=piece,
            dst_ref=piece,
            send_sem=sem,
            recv_sem=arrived_sem,
            device_id={"pool": device},
            device_id_type=MESH,
        )

    def arrive(zz, yy, cc):
        copy(zz, yy, cc, core_sem.at[0], twin).wait_recv()

    def column(zz, act):
        @pl.when((zz <= z) & has_up)
        def _():
            act(copy(zz, y, c, up_sem.at[zz], above))

        @pl.when((zz >= z) & has_down)
        def _():
            act(copy(zz, y, c, down_sem.at[zz], below))

        @pl.when((edge & (zz != far_z)) | (middle & (zz != edge_z)))
        def _():
            act(copy(zz, y, c, y_sem.at[zz], across))

        @pl.when(edge & (zz == far_z))
        def _():
            slot = slot_of(zz, y, c)
            act(half_copy(zz, 0, y_sem.at[zz], recv_sem.at[slot], across, y))

        act(copy(zz, y, c, core_sem.at[zz * 2 + y], twin))

    def extra(zz, act):
        @pl.when(edge & (zz == edge_z))
        def _():
            act(copy(zz, 1 - y, c, extra_sem, mate))

        @pl.when(middle & (zz == far_z))
        def _():
            act(half_copy(zz, 1, extra_sem, half_sem, mate, 1 - y))

    def arrive_side(zz):
        @pl.when((zz != far_z) | middle)
        def _():
            arrive(zz, 1 - y, c)

        @pl.when(edge & (zz == far_z))
        def _():
            slot = slot_of(zz, 1 - y, c)
            half_copy(zz, 0, extra_sem, recv_sem.at[slot], mate, 1 - y).wait_recv()
            half_copy(zz, 1, extra_sem, half_sem, mate, 1 - y).wait_recv()

    def work(slot):
        block = keys.at[slot]
        fetched = (
            pltpu.make_async_copy(lq.at[slot], lq_now, lq_sem),
            pltpu.make_async_copy(pq.at[slot], pq_now, pq_sem),
        )
        for item in fetched:
            item.start()
        for item in fetched:
            item.wait()
        result = attend_one(
            lq_now[...], pq_now[...], block, hits[slot], misses[slot], key_count, miss_rows
        ).astype(context.dtype)
        place = pl.ds(pl.multiple_of(slot * miss_rows, miss_rows), miss_rows)
        for head in range(result.shape[0] // miss_rows):
            context_now[:, head * LATENT_WIDTH : (head + 1) * LATENT_WIDTH] = result[
                head * miss_rows : (head + 1) * miss_rows
            ]
        stored = pltpu.make_async_copy(context_now, context.at[place], context_sem)
        stored.start()
        wide = -(-key_count // PACK) * PACK
        chosen = rows_sel[slot] == lax.broadcasted_iota(
            jnp.int32, (rows_sel.shape[1], wide), 1
        )
        chosen = chosen.astype(jnp.bfloat16)
        latent = jnp.dot(
            chosen[:, :key_count], block[:key_count, :], preferred_element_type=jnp.float32
        )
        sums = [jnp.zeros((rows_sel.shape[1], 128), jnp.float32)] * 2
        for chunk in range(wide // PACK):
            pair = chunk // 2
            sums[chunk % 2] += jnp.dot(
                chosen[:, chunk * PACK : (chunk + 1) * PACK],
                block[key_count:, pair * 128 : (pair + 1) * 128],
                preferred_element_type=jnp.float32,
            )
        rotary = sums[0][:, :ROPE] + sums[1][:, ROPE:]
        pages[slot, :, :LATENT_WIDTH] = latent.astype(pages.dtype)
        pages[slot, :, LATENT_WIDTH:] = rotary.astype(pages.dtype)
        stored.wait()

    def place_of(distance, way):
        zz = z + jnp.where(way == 0, -distance, distance)
        inside = (zz >= 0) & (zz <= 3) & (distance >= 0) & (distance <= 3)
        return jnp.clip(zz, 0, 3), inside & ((distance > 0) | (way == 0))

    def step(distance, carry):
        for way in range(2):
            zz, inside = place_of(distance, way)

            @pl.when(inside)
            def _():
                @pl.when(distance > 0)
                def _():
                    arrive(zz, y, c)

                column(zz, lambda item: item.start())

        for way in range(2):
            zz, inside = place_of(distance - 1, way)

            @pl.when(inside)
            def _():
                arrive_side(zz)
                extra(zz, lambda item: item.start())
                copy(zz, 1 - y, c, core_sem.at[zz * 2 + 1 - y], twin).start()

        def one(index, carry):
            way = lax.rem(index, 2)
            cc = lax.rem(c + lax.rem(index // 2, 2), 2)
            side = index // 4
            yy = lax.rem(y + side, 2)
            zz, inside = place_of(distance - side, way)

            @pl.when(inside)
            def _():
                @pl.when(cc != c)
                def _():
                    arrive(zz, yy, cc)

                work(slot_of(zz, yy, cc))

            return carry

        return lax.fori_loop(0, 8, one, carry)

    lax.fori_loop(0, 5, step, 0)

    def finish(zz, carry):
        column(zz, lambda item: item.wait_send())
        extra(zz, lambda item: item.wait_send())
        copy(zz, 1 - y, c, core_sem.at[zz * 2 + 1 - y], twin).wait_send()
        return carry

    lax.fori_loop(0, 4, finish, 0)


def serve(own, latent_queries, paired_queries, hits, misses, picks, key_count, miss_rows):
    prompts, rows, _ = latent_queries.shape
    heads = rows // miss_rows
    picked = picks[:, :, None] * PAGE + jnp.arange(PAGE)
    picked = jnp.where(picks[:, :, None] >= 0, picked, -1).reshape(prompts, -1, 1)
    vmem = pl.BlockSpec(memory_space=pltpu.VMEM)
    smem = pl.BlockSpec(memory_space=pltpu.SMEM)
    away = pl.BlockSpec(memory_space=pl.ANY)
    return pl.pallas_call(
        functools.partial(serve_body, key_count, miss_rows),
        out_shape=[
            jax.ShapeDtypeStruct((prompts * miss_rows, heads * LATENT_WIDTH), jnp.bfloat16),
            jax.ShapeDtypeStruct((prompts, picked.shape[1], LATENT_WIDTH + ROPE), jnp.bfloat16),
        ],
        in_specs=[smem, smem, away, away, away, vmem],
        out_specs=[away, vmem],
        scratch_shapes=[
            pltpu.VMEM((TPW,) + own.shape, own.dtype),
            pltpu.VMEM(latent_queries.shape[1:], own.dtype),
            pltpu.VMEM(paired_queries.shape[1:], own.dtype),
            pltpu.VMEM((miss_rows, heads * LATENT_WIDTH), jnp.bfloat16),
            pltpu.SemaphoreType.DMA,
            pltpu.SemaphoreType.DMA,
            pltpu.SemaphoreType.DMA,
            pltpu.SemaphoreType.DMA,
            pltpu.SemaphoreType.DMA((4,)),
            pltpu.SemaphoreType.DMA((4,)),
            pltpu.SemaphoreType.DMA((4,)),
            pltpu.SemaphoreType.DMA((8,)),
            pltpu.SemaphoreType.DMA,
            pltpu.SemaphoreType.DMA,
            pltpu.SemaphoreType.DMA((TPW,)),
        ],
        compiler_params=pltpu.CompilerParams(
            collective_id=0, has_side_effects=True, vmem_limit_bytes=24 * 1024 * 1024
        ),
    )(hits, misses, own, latent_queries, paired_queries, picked)


def shards(
    queries,
    pool_cache,
    new_raw,
    norm_gain,
    hit_pages,
    prompt_len,
    page_holder,
    page_slot,
    page_owner,
):
    pool_size = lax.axis_size("pool")
    device_index = lax.axis_index("pool")
    pages_max = page_holder.shape[1]
    slot_cap = max(2, 2 * pages_max // pool_size)
    features = pool_cache.shape[1] // PAGE
    misses = prompt_len - PAGE * hit_pages
    page_steps = jnp.arange(pages_max)
    page_live = page_steps[None, :] < hit_pages[:, None]
    held_here = page_live & (page_holder == device_index)
    held_rank = jnp.cumsum(held_here.astype(jnp.int32), axis=1) - 1
    cap_steps = jnp.arange(slot_cap)
    chosen = held_here[:, None, :] & (held_rank[:, None, :] == cap_steps[None, :, None])
    slot_index = jnp.sum(jnp.where(chosen, page_slot[:, None, :], 0), axis=2).reshape(-1)
    outbox = pool_cache[slot_index]
    arrived = lax.all_to_all(outbox, "pool", split_axis=0, concat_axis=0, tiled=True)
    own_hit = hit_pages[device_index]
    own_miss = misses[device_index]
    own_holder = page_holder[device_index]
    own_owner = page_owner[device_index, :, 0]
    own_live = page_steps < own_hit
    before = (
        (page_steps[None, :] < page_steps[:, None])
        & (own_holder[None, :] == own_holder[:, None])
        & own_live[None, :]
    )
    page_rank = jnp.sum(before.astype(jnp.int32), axis=1)
    source = jnp.where(own_live, own_holder * slot_cap + page_rank, 0)
    cached_pages = arrived[source]
    new_rows = new_raw.shape[0] * PAGE
    new_keys = fresh_keys(
        new_raw.astype(jnp.float32).reshape(new_rows, features), norm_gain, own_hit, own_miss
    )
    new_pages = new_keys.reshape(-1, PAGE * features)
    per_prompt = new_pages.shape[0]
    total = pages_max + per_prompt
    push_cap = max(2, (total + pool_size - 1) // pool_size)
    slot_total = pool_size * push_cap
    new_steps = jnp.arange(per_prompt)
    own_keys = jnp.concatenate([cached_pages.reshape(pages_max * PAGE, features), new_keys], axis=0)
    member = device_index % TPW
    group_base = device_index - member
    group_hits = lax.dynamic_slice_in_dim(hit_pages, group_base, TPW)
    group_misses = lax.dynamic_slice_in_dim(misses, group_base, TPW)
    head_dev = queries.shape[2] // features
    query_rows = queries.reshape(TPW, -1, head_dev, features)
    miss_rows = query_rows.shape[1]
    latent_queries, paired_queries = turn_queries(query_rows, group_hits)
    group_owner = lax.dynamic_slice_in_dim(page_owner[:, :, 0], group_base, TPW)
    group_live = jnp.concatenate(
        [page_steps < group_hits[:, None], new_steps * PAGE < group_misses[:, None]], axis=1
    )
    taken = group_live & (group_owner == device_index)
    rank = jnp.cumsum(taken.astype(jnp.int32), axis=1) - 1
    all_steps = jnp.arange(total)
    hit = taken[:, None, :] & (rank[:, None, :] == jnp.arange(push_cap)[None, :, None])
    picks = jnp.sum(jnp.where(hit, all_steps + 1, 0), axis=2) - 1
    context, pages = serve(
        pack_keys(own_keys),
        latent_queries,
        paired_queries,
        group_hits,
        group_misses,
        picks,
        own_keys.shape[0],
        miss_rows,
    )
    if pool_size == TPW:
        delivered = pages.reshape(slot_total, PAGE * features)
    else:
        all_live = jnp.concatenate([own_live, new_steps * PAGE < own_miss], axis=0)
        same_owner = (
            (all_steps[None, :] < all_steps[:, None])
            & (own_owner[None, :] == own_owner[:, None])
            & all_live[None, :]
        )
        slot_position = own_owner * push_cap + jnp.sum(same_owner.astype(jnp.int32), axis=1)
        every_page = jnp.concatenate([cached_pages, new_pages], axis=0)
        outgoing = pick_rows(slot_position, all_live, every_page, slot_total)
        delivered = lax.all_to_all(outgoing, "pool", split_axis=0, concat_axis=0, tiled=True)
    return (context[None], delivered)


def solution(mesh):
    in_specs = (
        P(("groups", "pool"), None, None),
        P(("groups", "pool"), None),
        P(("groups", "pool"), None),
        P(),
        P("groups"),
        P("groups"),
        P("groups", None),
        P("groups", None),
        P("groups", None, None),
    )
    out_specs = (P(("groups", "pool"), None, None), P(("groups", "pool"), None))
    return jax.shard_map(shards, mesh=mesh, in_specs=in_specs, out_specs=out_specs, check_vma=False)
```

```python
import functools

import jax
import jax.numpy as jnp
from jax import lax
from jax.experimental import pallas as pl
from jax.experimental.pallas import tpu as pltpu
from jax.sharding import PartitionSpec as P

LATENT_WIDTH = 512
ROPE = 64
PAGE = 16
TPW = 16
PACK = 128
MESH = pl.DeviceIdType.MESH


score_scale = 0.07216878364870323
rope_base = 10000.0
norm_eps = 1e-06


def rope_tables(positions, rotary_width):
    half_width = rotary_width // 2
    frequencies = rope_base ** (jnp.arange(half_width).astype(jnp.float32) * (-2.0 / rotary_width))
    angles = positions.astype(jnp.float32)[:, None] * frequencies[None, :]
    return (jnp.cos(angles), jnp.sin(angles))


def rotate(values, cosine, sine_table):
    half_width = values.shape[-1] // 2
    lower = values[..., :half_width]
    upper = values[..., half_width:]
    return jnp.concatenate(
        [lower * cosine - upper * sine_table, upper * cosine + lower * sine_table], axis=-1
    )


def fresh_keys(raw_rows, norm_gain, hit_count, miss_count):
    latent = raw_rows[:, :LATENT_WIDTH]
    rotary = raw_rows[:, LATENT_WIDTH:]
    mean_square = jnp.mean(latent * latent, axis=1, keepdims=True)
    normed = latent * lax.rsqrt(mean_square + norm_eps) * norm_gain.astype(jnp.float32)[None, :]
    row_steps = jnp.arange(raw_rows.shape[0])
    cosine, sine_table = rope_tables(hit_count * PAGE + row_steps, ROPE)
    turned = rotate(rotary, cosine, sine_table)
    joined = jnp.concatenate([normed, turned], axis=1)
    return jnp.where((row_steps < miss_count)[:, None], joined, 0.0).astype(jnp.bfloat16)


def pick_rows(slot_position, valid_rows, rows, slot_total):
    selector = (jnp.arange(slot_total)[:, None] == slot_position[None, :]) & valid_rows[None, :]
    return jnp.dot(selector.astype(jnp.bfloat16), rows, preferred_element_type=jnp.float32).astype(
        jnp.bfloat16
    )


def turn_queries(query_rows, hits):
    batch, miss_rows = (query_rows.shape[0], query_rows.shape[1])
    row_steps = jnp.arange(miss_rows)
    positions = (hits[:, None] * PAGE + row_steps[None, :]).reshape(-1)
    cosine, sine_table = rope_tables(positions, ROPE)
    cosine = cosine.reshape(batch, miss_rows, 1, -1)
    sine_table = sine_table.reshape(batch, miss_rows, 1, -1)
    turned = rotate(query_rows[..., LATENT_WIDTH:].astype(jnp.float32), cosine, sine_table).astype(
        jnp.bfloat16
    )
    by_head = lambda value: value.transpose(0, 2, 1, 3).reshape(batch, -1, value.shape[-1])
    latent = by_head(query_rows[..., :LATENT_WIDTH])
    rotary = by_head(turned)
    blank = jnp.zeros_like(rotary)
    paired = jnp.concatenate(
        [jnp.concatenate([rotary, blank], axis=2), jnp.concatenate([blank, rotary], axis=2)], axis=1
    )
    return latent, paired


def pack_keys(keys):
    rotary = keys[:, LATENT_WIDTH:]
    spare = PACK * (LATENT_WIDTH // ROPE) - keys.shape[0]
    rotary = jnp.concatenate([rotary, jnp.zeros((spare, ROPE), keys.dtype)], axis=0)
    packed = rotary.reshape(-1, PACK, ROPE).transpose(1, 0, 2).reshape(PACK, LATENT_WIDTH)
    return jnp.concatenate([keys[:, :LATENT_WIDTH], packed], axis=0)


def attend_one(latent_queries, paired_queries, keys, hits, misses, key_count, miss_rows):
    rows = latent_queries.shape[0]
    cached_rows = key_count - miss_rows
    contract = (((1,), (1,)), ((), ()))
    latent_keys = keys[:key_count, :]
    scores = lax.dot_general(
        latent_queries, latent_keys, contract, preferred_element_type=jnp.float32
    )
    parts = []
    for pair in range(LATENT_WIDTH // 128):
        if pair * 2 * PACK >= key_count:
            break
        both = lax.dot_general(
            paired_queries,
            keys[key_count:, pair * 128 : (pair + 1) * 128],
            contract,
            preferred_element_type=jnp.float32,
        )
        parts += [both[:rows], both[rows:]]
    rotary = jnp.concatenate(parts, axis=1)[:, :key_count]
    scores = (scores + rotary) * score_scale
    row_steps = lax.rem(lax.broadcasted_iota(jnp.int32, (rows, 1), 0), miss_rows)
    key_steps = lax.broadcasted_iota(jnp.int32, (rows, key_count), 1)
    fresh_end = cached_rows + jnp.minimum(row_steps + 1, misses)
    allowed = (key_steps < hits * PAGE) | ((key_steps >= cached_rows) & (key_steps < fresh_end))
    scores = jnp.where(allowed, scores, -jnp.inf)
    row_max = jnp.max(scores, axis=1, keepdims=True)
    weights = jnp.exp(scores - row_max)
    total = jnp.sum(weights, axis=1, keepdims=True)
    context = jnp.dot(
        weights.astype(jnp.bfloat16), latent_keys, preferred_element_type=jnp.float32
    )
    return jnp.where(row_steps < misses, context / total, 0.0)


def serve_body(
    key_count, miss_rows, hits, misses, own, lq, pq, rows_sel, context, pages, keys, *scratch
):
    lq_now, pq_now, context_now, lq_sem, pq_sem, context_sem = scratch[:6]
    local_sem, up_sem, down_sem, y_sem, core_sem, extra_sem, half_sem, recv_sem = scratch[6:]
    me = lax.axis_index("pool")
    member = lax.rem(me, TPW)
    base = me - member
    z, y, c = member // 4, lax.rem(member // 2, 2), lax.rem(member, 2)

    def slot_of(zz, yy, cc):
        return zz * 4 + yy * 2 + cc

    across = base + slot_of(z, 1 - y, c)
    twin = base + slot_of(z, y, 1 - c)
    above = base + slot_of(lax.rem(z + 1, 4), y, c)
    below = base + slot_of(lax.rem(z + 3, 4), y, c)
    has_up, has_down = z < 3, z > 0
    edge_z = jnp.where(z < 2, 0, 3)
    far_z = 3 - edge_z
    edge = z == edge_z
    middle = z != edge_z
    mate = base + slot_of(z + 1 - 2 * lax.rem(z, 2), y, c)
    half_rows = own.shape[0] // 2

    barrier = pltpu.get_barrier_semaphore()
    pl.semaphore_signal(barrier, inc=1, device_id={"pool": across}, device_id_type=MESH)
    pl.semaphore_signal(barrier, inc=1, device_id={"pool": twin}, device_id_type=MESH)

    @pl.when(has_up)
    def _():
        pl.semaphore_signal(barrier, inc=1, device_id={"pool": above}, device_id_type=MESH)

    @pl.when(has_down)
    def _():
        pl.semaphore_signal(barrier, inc=1, device_id={"pool": below}, device_id_type=MESH)

    mine = pltpu.make_async_copy(own, keys.at[member], local_sem)
    mine.start()
    pl.semaphore_wait(barrier, 2 + has_up.astype(jnp.int32) + has_down.astype(jnp.int32))
    mine.wait()

    def copy(zz, yy, cc, sem, device):
        slot = slot_of(zz, yy, cc)
        return pltpu.make_async_remote_copy(
            src_ref=keys.at[slot],
            dst_ref=keys.at[slot],
            send_sem=sem,
            recv_sem=recv_sem.at[slot],
            device_id={"pool": device},
            device_id_type=MESH,
        )

    def half_copy(zz, part, sem, arrived_sem, device, yy):
        piece = keys.at[slot_of(zz, yy, c), pl.ds(part * half_rows, half_rows)]
        return pltpu.make_async_remote_copy(
            src_ref=piece,
            dst_ref=piece,
            send_sem=sem,
            recv_sem=arrived_sem,
            device_id={"pool": device},
            device_id_type=MESH,
        )

    def arrive(zz, yy, cc):
        copy(zz, yy, cc, core_sem.at[0], twin).wait_recv()

    def column(zz, act):
        @pl.when((zz <= z) & has_up)
        def _():
            act(copy(zz, y, c, up_sem.at[zz], above))

        @pl.when((zz >= z) & has_down)
        def _():
            act(copy(zz, y, c, down_sem.at[zz], below))

        @pl.when((edge & (zz != far_z)) | (middle & (zz != edge_z)))
        def _():
            act(copy(zz, y, c, y_sem.at[zz], across))

        @pl.when(edge & (zz == far_z))
        def _():
            slot = slot_of(zz, y, c)
            act(half_copy(zz, 0, y_sem.at[zz], recv_sem.at[slot], across, y))

        act(copy(zz, y, c, core_sem.at[zz * 2 + y], twin))

    def extra(zz, act):
        @pl.when(edge & (zz == edge_z))
        def _():
            act(copy(zz, 1 - y, c, extra_sem, mate))

        @pl.when(middle & (zz == far_z))
        def _():
            act(half_copy(zz, 1, extra_sem, half_sem, mate, 1 - y))

    def arrive_side(zz):
        @pl.when((zz != far_z) | middle)
        def _():
            arrive(zz, 1 - y, c)

        @pl.when(edge & (zz == far_z))
        def _():
            slot = slot_of(zz, 1 - y, c)
            half_copy(zz, 0, extra_sem, recv_sem.at[slot], mate, 1 - y).wait_recv()
            half_copy(zz, 1, extra_sem, half_sem, mate, 1 - y).wait_recv()

    def work(slot):
        block = keys.at[slot]
        fetched = (
            pltpu.make_async_copy(lq.at[slot], lq_now, lq_sem),
            pltpu.make_async_copy(pq.at[slot], pq_now, pq_sem),
        )
        for item in fetched:
            item.start()
        for item in fetched:
            item.wait()
        result = attend_one(
            lq_now[...], pq_now[...], block, hits[slot], misses[slot], key_count, miss_rows
        ).astype(context.dtype)
        place = pl.ds(pl.multiple_of(slot * miss_rows, miss_rows), miss_rows)
        for head in range(result.shape[0] // miss_rows):
            context_now[:, head * LATENT_WIDTH : (head + 1) * LATENT_WIDTH] = result[
                head * miss_rows : (head + 1) * miss_rows
            ]
        stored = pltpu.make_async_copy(context_now, context.at[place], context_sem)
        stored.start()
        wide = -(-key_count // PACK) * PACK
        chosen = rows_sel[slot] == lax.broadcasted_iota(
            jnp.int32, (rows_sel.shape[1], wide), 1
        )
        chosen = chosen.astype(jnp.bfloat16)
        latent = jnp.dot(
            chosen[:, :key_count], block[:key_count, :], preferred_element_type=jnp.float32
        )
        sums = [jnp.zeros((rows_sel.shape[1], 128), jnp.float32)] * 2
        for chunk in range(wide // PACK):
            pair = chunk // 2
            sums[chunk % 2] += jnp.dot(
                chosen[:, chunk * PACK : (chunk + 1) * PACK],
                block[key_count:, pair * 128 : (pair + 1) * 128],
                preferred_element_type=jnp.float32,
            )
        rotary = sums[0][:, :ROPE] + sums[1][:, ROPE:]
        pages[slot, :, :LATENT_WIDTH] = latent.astype(pages.dtype)
        pages[slot, :, LATENT_WIDTH:] = rotary.astype(pages.dtype)
        stored.wait()

    def place_of(distance, way):
        zz = z + jnp.where(way == 0, -distance, distance)
        inside = (zz >= 0) & (zz <= 3) & (distance >= 0) & (distance <= 3)
        return jnp.clip(zz, 0, 3), inside & ((distance > 0) | (way == 0))

    def step(distance, carry):
        for way in range(2):
            zz, inside = place_of(distance, way)

            @pl.when(inside)
            def _():
                @pl.when(distance > 0)
                def _():
                    arrive(zz, y, c)

                column(zz, lambda item: item.start())

        for way in range(2):
            zz, inside = place_of(distance - 1, way)

            @pl.when(inside)
            def _():
                arrive_side(zz)
                extra(zz, lambda item: item.start())
                copy(zz, 1 - y, c, core_sem.at[zz * 2 + 1 - y], twin).start()

        def one(index, carry):
            way = lax.rem(index, 2)
            cc = lax.rem(c + lax.rem(index // 2, 2), 2)
            side = index // 4
            yy = lax.rem(y + side, 2)
            zz, inside = place_of(distance - side, way)

            @pl.when(inside)
            def _():
                @pl.when(cc != c)
                def _():
                    arrive(zz, yy, cc)

                work(slot_of(zz, yy, cc))

            return carry

        return lax.fori_loop(0, 8, one, carry)

    lax.fori_loop(0, 5, step, 0)

    def finish(zz, carry):
        column(zz, lambda item: item.wait_send())
        extra(zz, lambda item: item.wait_send())
        copy(zz, 1 - y, c, core_sem.at[zz * 2 + 1 - y], twin).wait_send()
        return carry

    lax.fori_loop(0, 4, finish, 0)


def serve(own, latent_queries, paired_queries, hits, misses, picks, key_count, miss_rows):
    prompts, rows, _ = latent_queries.shape
    heads = rows // miss_rows
    picked = picks[:, :, None] * PAGE + jnp.arange(PAGE)
    picked = jnp.where(picks[:, :, None] >= 0, picked, -1).reshape(prompts, -1, 1)
    vmem = pl.BlockSpec(memory_space=pltpu.VMEM)
    smem = pl.BlockSpec(memory_space=pltpu.SMEM)
    away = pl.BlockSpec(memory_space=pl.ANY)
    return pl.pallas_call(
        functools.partial(serve_body, key_count, miss_rows),
        out_shape=[
            jax.ShapeDtypeStruct((prompts * miss_rows, heads * LATENT_WIDTH), jnp.bfloat16),
            jax.ShapeDtypeStruct((prompts, picked.shape[1], LATENT_WIDTH + ROPE), jnp.bfloat16),
        ],
        in_specs=[smem, smem, away, away, away, vmem],
        out_specs=[away, vmem],
        scratch_shapes=[
            pltpu.VMEM((TPW,) + own.shape, own.dtype),
            pltpu.VMEM(latent_queries.shape[1:], own.dtype),
            pltpu.VMEM(paired_queries.shape[1:], own.dtype),
            pltpu.VMEM((miss_rows, heads * LATENT_WIDTH), jnp.bfloat16),
            pltpu.SemaphoreType.DMA,
            pltpu.SemaphoreType.DMA,
            pltpu.SemaphoreType.DMA,
            pltpu.SemaphoreType.DMA,
            pltpu.SemaphoreType.DMA((4,)),
            pltpu.SemaphoreType.DMA((4,)),
            pltpu.SemaphoreType.DMA((4,)),
            pltpu.SemaphoreType.DMA((8,)),
            pltpu.SemaphoreType.DMA,
            pltpu.SemaphoreType.DMA,
            pltpu.SemaphoreType.DMA((TPW,)),
        ],
        compiler_params=pltpu.CompilerParams(
            collective_id=0, has_side_effects=True, vmem_limit_bytes=58 * 1024 * 1024
        ),
    )(hits, misses, own, latent_queries, paired_queries, picked)


def shards(
    queries,
    pool_cache,
    new_raw,
    norm_gain,
    hit_pages,
    prompt_len,
    page_holder,
    page_slot,
    page_owner,
):
    pool_size = lax.axis_size("pool")
    device_index = lax.axis_index("pool")
    pages_max = page_holder.shape[1]
    slot_cap = max(2, 2 * pages_max // pool_size)
    features = pool_cache.shape[1] // PAGE
    misses = prompt_len - PAGE * hit_pages
    page_steps = jnp.arange(pages_max)
    page_live = page_steps[None, :] < hit_pages[:, None]
    held_here = page_live & (page_holder == device_index)
    held_rank = jnp.cumsum(held_here.astype(jnp.int32), axis=1) - 1
    cap_steps = jnp.arange(slot_cap)
    chosen = held_here[:, None, :] & (held_rank[:, None, :] == cap_steps[None, :, None])
    slot_index = jnp.sum(jnp.where(chosen, page_slot[:, None, :], 0), axis=2).reshape(-1)
    outbox = pool_cache[slot_index]
    arrived = lax.all_to_all(outbox, "pool", split_axis=0, concat_axis=0, tiled=True)
    own_hit = hit_pages[device_index]
    own_miss = misses[device_index]
    own_holder = page_holder[device_index]
    own_owner = page_owner[device_index, :, 0]
    own_live = page_steps < own_hit
    before = (
        (page_steps[None, :] < page_steps[:, None])
        & (own_holder[None, :] == own_holder[:, None])
        & own_live[None, :]
    )
    page_rank = jnp.sum(before.astype(jnp.int32), axis=1)
    source = jnp.where(own_live, own_holder * slot_cap + page_rank, 0)
    cached_pages = arrived[source]
    new_rows = new_raw.shape[0] * PAGE
    new_keys = fresh_keys(
        new_raw.astype(jnp.float32).reshape(new_rows, features), norm_gain, own_hit, own_miss
    )
    new_pages = new_keys.reshape(-1, PAGE * features)
    per_prompt = new_pages.shape[0]
    total = pages_max + per_prompt
    push_cap = max(2, (total + pool_size - 1) // pool_size)
    slot_total = pool_size * push_cap
    new_steps = jnp.arange(per_prompt)
    own_keys = jnp.concatenate([cached_pages.reshape(pages_max * PAGE, features), new_keys], axis=0)
    member = device_index % TPW
    group_base = device_index - member
    group_hits = lax.dynamic_slice_in_dim(hit_pages, group_base, TPW)
    group_misses = lax.dynamic_slice_in_dim(misses, group_base, TPW)
    head_dev = queries.shape[2] // features
    query_rows = queries.reshape(TPW, -1, head_dev, features)
    miss_rows = query_rows.shape[1]
    latent_queries, paired_queries = turn_queries(query_rows, group_hits)
    group_owner = lax.dynamic_slice_in_dim(page_owner[:, :, 0], group_base, TPW)
    group_live = jnp.concatenate(
        [page_steps < group_hits[:, None], new_steps * PAGE < group_misses[:, None]], axis=1
    )
    taken = group_live & (group_owner == device_index)
    rank = jnp.cumsum(taken.astype(jnp.int32), axis=1) - 1
    all_steps = jnp.arange(total)
    hit = taken[:, None, :] & (rank[:, None, :] == jnp.arange(push_cap)[None, :, None])
    picks = jnp.sum(jnp.where(hit, all_steps + 1, 0), axis=2) - 1
    context, pages = serve(
        pack_keys(own_keys),
        latent_queries,
        paired_queries,
        group_hits,
        group_misses,
        picks,
        own_keys.shape[0],
        miss_rows,
    )
    if pool_size == TPW:
        delivered = pages.reshape(slot_total, PAGE * features)
    else:
        all_live = jnp.concatenate([own_live, new_steps * PAGE < own_miss], axis=0)
        same_owner = (
            (all_steps[None, :] < all_steps[:, None])
            & (own_owner[None, :] == own_owner[:, None])
            & all_live[None, :]
        )
        slot_position = own_owner * push_cap + jnp.sum(same_owner.astype(jnp.int32), axis=1)
        every_page = jnp.concatenate([cached_pages, new_pages], axis=0)
        outgoing = pick_rows(slot_position, all_live, every_page, slot_total)
        delivered = lax.all_to_all(outgoing, "pool", split_axis=0, concat_axis=0, tiled=True)
    return (context[None], delivered)


def solution(mesh):
    in_specs = (
        P(("groups", "pool"), None, None),
        P(("groups", "pool"), None),
        P(("groups", "pool"), None),
        P(),
        P("groups"),
        P("groups"),
        P("groups", None),
        P("groups", None),
        P("groups", None, None),
    )
    out_specs = (P(("groups", "pool"), None, None), P(("groups", "pool"), None))
    return jax.shard_map(shards, mesh=mesh, in_specs=in_specs, out_specs=out_specs, check_vma=False)
```
